512 devices in a mesh: ens: 16 (over z, core), space: 32 (over y, x).
Axes of the slice: x: 4, y: 8, z: 8, core: 2. Of those that a mesh axis runs over, the one named last changes fastest.
Arguments:
- mesh_latent: bfloat16 [16, 4096, 512], P('ens', 'space'), may hold values from -6 to 6
- grid_embed: bfloat16 [16384, 512], P('space'), may hold values from -6 to 6
- w_send: bfloat16 [512, 512], replicated, may hold values from -0.25 to 0.25
- w_recv: bfloat16 [512, 512], replicated, may hold values from -0.25 to 0.25
- w_msg: bfloat16 [512, 512], replicated, may hold values from -0.25 to 0.25
- w_node: bfloat16 [512, 512], replicated, may hold values from -0.25 to 0.25
- w_out: bfloat16 [512, 100], replicated, may hold values from -0.25 to 0.25
- target: float32 [16384, 100], P('space'), may hold values from -6 to 6
- var_weight: float32 [100], replicated, may hold values from 0.5 to 4
- send_rows: int32 [32, 32, 8], P('space'), may hold values from 0 to 127
- edge_slot: int32 [16384, 4], P('space'), may hold values from 0 to 255
- edge_count: int32 [16384], P('space'), may hold values from 1 to 4
Outputs:
- mesh_grad: float32 [16, 4096, 512], P('ens', 'space')
- weight_grad: float32 [512, 512], P('space')
The draws below stay inside these ranges and needn't reach their ends.
Inputs may be any that keep to these rules, and one draw needn't show every extreme that they name: `send_rows`: local mesh row indices of the sending index of space. `edge_slot`: slots index the receiving device's 32 * 8 received rows, sender-major.
All inputs are finite; a program needn't handle non-finite values.
Results may differ from the reference program's by a relative error of at most 0.013.
Values may be sent and summed in bfloat16 or wider, within the bound.
A program may use at most 64 MiB of HBM per device.

```python
import math
import jax
import jax.numpy as jnp
from jax import lax

H = 512
V = 100
K = 4
GRID_DEV = 512
MESH_DEV = 128
CAP = 8
MEMBERS = 16
GRID = 16384
MESH = 4096
N_SPACE = 32


def with_ends(result, own_key, low, top_value):
    index_at = [jax.random.randint(jax.random.fold_in(own_key, axis), (), 0, length) for axis, length in enumerate(result.shape)]
    longest = result.shape.index(max(result.shape))
    next_to = index_at[:longest] + [(index_at[longest] + 1) % result.shape[longest]] + index_at[longest + 1:]
    return result.at[tuple(index_at)].set(low).at[tuple(next_to)].set(top_value)


def steps_of(stream_key, dims, shards, least, high):
    loudness = 1.0
    for position, shards_of in shards:
        draws = jax.random.uniform(jax.random.fold_in(jax.random.fold_in(stream_key, 6), position), (shards_of,), jnp.float32, least / len(shards), high / len(shards))
        loudness = loudness * jnp.repeat(jnp.exp(draws), dims[position] // shards_of).reshape((-1,) + (1,) * (len(dims) - 1 - position))
    return loudness


def scatter_about(own_key, shape, scale, reach, split=(), kind=jnp.bfloat16):
    entries = jax.random.normal(own_key, shape, jnp.float32) * scale
    if len(split) > 0:
        entries = steps_of(own_key, shape, split, -0.22, 0.18) * entries
    return jnp.clip(entries, min=-reach, max=reach).astype(kind)


def setup_inputs(seed: int = 0) -> dict:
    streams_of = jax.random.split(jax.random.key(seed), 13)
    mesh_latent = scatter_about(streams_of[0], (MEMBERS, MESH, H), 1.0, 6.0, ((0, 16), (1, 32)))
    grid_embed = scatter_about(streams_of[1], (GRID, H), 1.0, 6.0, ((0, 32),))
    w_send = scatter_about(streams_of[2], (H, H), H ** -0.5, 0.25)
    w_recv = scatter_about(streams_of[3], (H, H), H ** -0.5, 0.25)
    w_msg = scatter_about(streams_of[4], (H, H), H ** -0.5, 0.25)
    w_node = scatter_about(streams_of[5], (H, H), H ** -0.5, 0.25)
    w_out = scatter_about(streams_of[6], (H, V), H ** -0.5, 0.25)
    target = scatter_about(streams_of[7], (GRID, V), 1.0, 6.0, ((0, 32),), jnp.float32)
    var_weight = jnp.clip(jnp.exp(jax.random.uniform(streams_of[8], (V,), jnp.float32, math.log(0.5), math.log(4.0))), 0.5, 4.0)
    send_rows = with_ends(jax.random.randint(streams_of[9], (N_SPACE, N_SPACE, CAP), 0, MESH_DEV), jax.random.fold_in(streams_of[9], 1), 0, MESH_DEV - 1).astype(jnp.int32)
    edge_slot = with_ends(jax.random.randint(streams_of[10], (GRID, K), 0, N_SPACE * CAP), jax.random.fold_in(streams_of[10], 1), 0, (N_SPACE * CAP) - 1).astype(jnp.int32)
    edge_count = with_ends(jax.random.randint(streams_of[11], (GRID,), 1, K + 1), jax.random.fold_in(streams_of[11], 1), 1, K).astype(jnp.int32)
    return {"mesh_latent": mesh_latent, "grid_embed": grid_embed, "w_send": w_send, "w_recv": w_recv, "w_msg": w_msg, "w_node": w_node, "w_out": w_out, "target": target, "var_weight": var_weight, "send_rows": send_rows, "edge_slot": edge_slot, "edge_count": edge_count}


soft_square = 0.09

def silu_grad(value):
    logistic = jax.nn.sigmoid(value)
    return logistic * (1.0 + value * (1.0 - logistic))

def reference(mesh_latent, grid_embed, w_send, w_recv, w_msg, w_node, w_out, target, var_weight, send_rows, edge_slot, edge_count):
    base = jnp.arange(N_SPACE, dtype=jnp.int32)[:, None, None] * MESH_DEV + send_rows
    source = jnp.transpose(base, (1, 0, 2)).reshape(N_SPACE, N_SPACE * CAP)
    owners = jnp.arange(GRID, dtype=jnp.int32) // GRID_DEV
    edge_source = source[owners[:, None], edge_slot].astype(jnp.int32)
    live_mask = (jnp.arange(K, dtype=jnp.int32)[None, :] < edge_count[:, None]).astype(jnp.float32)
    grid_proj = jnp.dot(grid_embed, w_recv, preferred_element_type=jnp.float32)

    def forward(latent):
        projected = jnp.dot(latent, w_send, preferred_element_type=jnp.float32)
        preact = jnp.take(projected, edge_source.reshape(-1), axis=0).reshape(GRID, K, H) + grid_proj[:, None, :]
        activation = jax.nn.silu(preact).astype(jnp.bfloat16)
        messages = jnp.dot(activation.reshape(-1, H), w_msg, preferred_element_type=jnp.float32).reshape(GRID, K, H)
        summed = lax.optimization_barrier(jnp.sum(messages * live_mask[:, :, None], axis=1))
        node_in = (summed + grid_embed.astype(jnp.float32)).astype(jnp.bfloat16)
        node_pre = jnp.dot(node_in, w_node, preferred_element_type=jnp.float32)
        hidden = jax.nn.silu(node_pre).astype(jnp.bfloat16)
        pred = jnp.dot(hidden, w_out, preferred_element_type=jnp.float32)
        return (pred, preact, activation, node_pre)
    preds = lax.map(lambda latent: forward(latent)[0], mesh_latent)
    members = preds.shape[0]

    def add_pair(total, other):
        spread = preds - other[None]
        return (total + spread / jnp.sqrt(spread * spread + soft_square), None)
    pairwise, _ = lax.scan(add_pair, jnp.zeros_like(preds), preds)
    target_gap = preds - target[None]
    pred_grad = (var_weight * (target_gap / jnp.sqrt(target_gap * target_gap + soft_square) - pairwise / (members - 1.0))).astype(jnp.bfloat16)

    def backward(member_item):
        latent, member_grad = member_item
        pred, preact, activation, node_pre = forward(latent)
        hidden_grad = (jnp.dot(member_grad, w_out.T, preferred_element_type=jnp.float32) * silu_grad(node_pre)).astype(jnp.bfloat16)
        edge_grad = jnp.dot(hidden_grad, w_node.T, preferred_element_type=jnp.float32).astype(jnp.bfloat16)
        message_grad = (edge_grad[:, None, :].astype(jnp.float32) * live_mask[:, :, None]).astype(jnp.bfloat16).reshape(-1, H)
        preact_grad = (jnp.dot(message_grad, w_msg.T, preferred_element_type=jnp.float32).reshape(GRID, K, H) * silu_grad(preact)).astype(jnp.bfloat16)
        weight_term = lax.dot_general(activation.reshape(-1, H), message_grad, (((0,), (0,)), ((), ())), preferred_element_type=jnp.float32)
        row_grads = jax.ops.segment_sum(preact_grad.reshape(-1, H).astype(jnp.float32), edge_source.reshape(-1), num_segments=MESH)
        member_mesh = jnp.dot(row_grads, w_send.astype(jnp.float32).T, precision=lax.Precision.HIGHEST)
        return (member_mesh, weight_term)
    mesh_grad, weight_terms = lax.map(backward, (mesh_latent, pred_grad))
    weight_grad = lax.optimization_barrier(jnp.sum(weight_terms, axis=0)) * (1.0 / math.sqrt(members * GRID * K))
    return (mesh_grad, weight_grad)
```

```python
import functools
import math

import jax
import jax.numpy as jnp
from jax import lax
from jax.experimental import pallas as pl
from jax.experimental.pallas import tpu as pltpu
from jax.sharding import PartitionSpec as P

MESH = pl.DeviceIdType.MESH
F32 = jnp.float32
BF16 = jnp.bfloat16
SOFT = 0.09
LANES = 128


def sigmoid(v):
    return 0.5 * jnp.tanh(0.5 * v) + 0.5


def dot(a, b):
    return jnp.dot(a, b, preferred_element_type=F32)


def dot_t(a, b):
    return lax.dot_general(a, b, (((1,), (1,)), ((), ())), preferred_element_type=F32)


def to_blocks(rows, n):
    c, f = rows.shape[0] // n, rows.shape[1]
    split = rows.reshape(n, c, f)
    return jnp.concatenate([split[:, :, : f // 2], split[:, :, f // 2 :]], axis=1)


def from_blocks(blocks):
    n, c2, f2 = blocks.shape
    c = c2 // 2
    left = blocks[:, :c, :].reshape(n * c, f2)
    right = blocks[:, c:, :].reshape(n * c, f2)
    return jnp.concatenate([left, right], axis=1)


def kernel(
    n_ens,
    n_sp,
    scale,
    lat_h,
    emb_h,
    w_send_h,
    w_recv_h,
    w_msg_h,
    w_node_h,
    w_out_h,
    target_h,
    var_ref,
    rows_ref,
    slot_ref,
    count_ref,
    mesh_ref,
    weight_ref,
    lat,
    emb,
    w_send,
    w_recv,
    w_msg,
    w_node,
    w_out_raw,
    target_raw,
    w_out_wide,
    w_out,
    target_wide,
    target,
    small,
    columns,
    pick,
    pick_t,
    out_rows,
    in_rows,
    slot_proj,
    grid_proj,
    one_hot,
    one_hot_t,
    pre,
    live,
    summed_act,
    summed_act_t,
    node_pre,
    pred,
    pred_in,
    grad_wide,
    grad_out,
    grad_in,
    pred_grad,
    edge_grad,
    back,
    pre_grad,
    own_half,
    pair_out,
    pair_in,
    z_out,
    z_in,
    part_out,
    part_in,
    total_out,
    total_in,
    rows_out,
    rows_in,
    load_sem,
    send_sem,
    recv_sem,
):
    ens = lax.axis_index("ens")
    sp = lax.axis_index("space")
    n_z = n_ens // 2
    core = lax.rem(ens, 2)
    z = lax.div(ens, 2)
    points, features = emb.shape
    per_point = slot_ref.shape[0]
    cap = rows_ref.shape[0]
    slots = n_sp * cap
    chunk = points // n_ens
    half = features // 2
    block = features // n_ens
    out_block = features // n_sp
    per_block = n_sp // n_ens

    loads = [
        pltpu.make_async_copy(src, dst, load_sem.at[i])
        for i, (src, dst) in enumerate(
            [
                (lat_h, lat),
                (emb_h, emb),
                (w_recv_h, w_recv),
                (w_send_h, w_send),
                (w_msg_h, w_msg),
                (w_node_h, w_node),
                (w_out_h, w_out_raw),
                (target_h, target_raw),
            ]
        )
    ]
    for load in loads:
        load.start()

    barrier = pltpu.get_barrier_semaphore()

    @pl.loop(1, n_sp)
    def _(q):
        pl.semaphore_signal(
            barrier, inc=1, device_id={"space": lax.rem(sp + q, n_sp)}, device_id_type=MESH
        )

    @pl.loop(1, n_ens)
    def _(q):
        pl.semaphore_signal(
            barrier, inc=1, device_id={"ens": lax.rem(ens + q, n_ens)}, device_id_type=MESH
        )

    def exchange(src, dst, which, axis, me, n):
        @pl.loop(1, n)
        def _(q):
            pltpu.make_async_remote_copy(
                src_ref=src.at[q],
                dst_ref=dst.at[n - q],
                send_sem=send_sem.at[which],
                recv_sem=recv_sem.at[which],
                device_id={axis: lax.rem(me + q, n)},
                device_id_type=MESH,
            ).start()

    def whole(ref, which):
        return pltpu.make_async_remote_copy(
            src_ref=ref,
            dst_ref=ref,
            send_sem=send_sem.at[which],
            recv_sem=recv_sem.at[which],
            device_id={"ens": ens},
            device_id_type=MESH,
        )

    tiled = jnp.broadcast_to(
        rows_ref[...].astype(F32)[None], (n_sp, cap, n_sp)
    ).reshape(slots, n_sp)
    place = lax.broadcasted_iota(jnp.int32, (slots, n_sp), 0) // cap + sp
    place = jnp.where(place >= n_sp, place - n_sp, place)
    lane = lax.broadcasted_iota(jnp.int32, (slots, n_sp), 1)
    wanted = jnp.sum(jnp.where(lane == place, tiled, 0.0), axis=1, keepdims=True)
    local_rows = lat.shape[0]
    pick_wide = jnp.where(
        lax.broadcasted_iota(jnp.int32, (slots, local_rows), 1).astype(F32) == wanted, 1.0, 0.0
    )
    pick[...] = pick_wide.astype(BF16)
    loads[0].wait()
    blocks = to_blocks(dot(pick[...], lat[...]), n_sp).astype(BF16)
    out_rows[...] = blocks
    in_rows[0] = blocks[0]
    pl.semaphore_wait(barrier, n_sp + n_ens - 2)
    exchange(out_rows, in_rows, 0, "space", sp, n_sp)

    loads[1].wait()
    loads[2].wait()
    grid_proj[...] = dot(emb[...], w_recv[...])
    pick_t[...] = jnp.transpose(pick_wide).astype(BF16)
    slot = slot_ref[...] - cap * sp
    slot = jnp.where(slot < 0, slot + slots, slot)
    is_live = lax.broadcasted_iota(jnp.int32, slot.shape, 0) < count_ref[...]
    small[...] = jnp.zeros_like(small)
    small[0:per_point, :] = slot.astype(F32)
    small[per_point : 2 * per_point, :] = jnp.where(is_live, 1.0, 0.0)
    columns[...] = jnp.transpose(small[...])
    slot = jnp.where(is_live, slot, -1)
    slot_index = lax.broadcasted_iota(jnp.int32, (slots, points), 0)
    lane_index = lax.broadcasted_iota(jnp.int32, (points, slots), 1).astype(F32)
    for k in range(per_point):
        one_hot[k] = jnp.where(lane_index == columns[:, k : k + 1], 1.0, 0.0).astype(BF16)
        one_hot_t[:, k * points : (k + 1) * points] = jnp.where(
            slot_index == slot[k : k + 1, :], 1.0, 0.0
        ).astype(BF16)
        live[k] = jnp.broadcast_to(
            columns[:, per_point + k : per_point + k + 1], (points, LANES)
        )
    loads[6].wait()
    variables = w_out_raw.shape[0]
    w_out_wide[...] = jnp.zeros_like(w_out_wide)
    w_out_wide[0:variables, :] = w_out_raw[...].astype(F32)
    w_out[...] = w_out_wide[...].astype(BF16)
    loads[7].wait()
    target_wide[...] = jnp.zeros_like(target_wide)
    target_wide[0:variables, :] = target_raw[...]
    target[...] = jnp.transpose(target_wide[...])
    loads[3].wait()
    loads[4].wait()
    loads[5].wait()

    whole(in_rows.at[pl.ds(1, n_sp - 1)], 0).wait_recv()
    arrived = from_blocks(in_rows[...].astype(F32)).astype(BF16)
    slot_proj[...] = dot(arrived, w_send[...]).astype(BF16)
    for k in range(per_point):
        pre[k] = dot(one_hot[k], slot_proj[...])

    step = 16

    def spread(k, rows):
        return jnp.concatenate([live[k, rows, :]] * (features // LANES), axis=1)

    @pl.loop(0, points // step)
    def _(i):
        rows = pl.ds(pl.multiple_of(i * step, step), step)
        base = grid_proj[rows, :]
        total = jnp.zeros((step, features), F32)
        for k in range(per_point):
            v = pre[k, rows, :] + base
            total += v * sigmoid(v) * spread(k, rows)
        summed_act[rows, :] = total.astype(BF16)

    node_in = (dot(summed_act[...], w_msg[...]) + emb[...].astype(F32)).astype(BF16)
    node_pre[...] = dot(node_in, w_node[...])
    v = node_pre[...]
    hidden = (v * sigmoid(v)).astype(BF16)
    pred[...] = dot_t(hidden, w_out[...]).reshape(pred.shape)

    pred_in[0] = pred[ens]

    @pl.loop(1, n_ens)
    def _(q):
        to = lax.rem(ens + q, n_ens)
        pltpu.make_async_remote_copy(
            src_ref=pred.at[to],
            dst_ref=pred_in.at[n_ens - q],
            send_sem=send_sem.at[1],
            recv_sem=recv_sem.at[1],
            device_id={"ens": to},
            device_id_type=MESH,
        ).start()

    @pl.loop(0, points // step)
    def _(i):
        rows = pl.ds(pl.multiple_of(i * step, step), step)
        base = grid_proj[rows, :]
        for k in range(per_point):
            v = pre[k, rows, :] + base
            s = sigmoid(v)
            pre[k, rows, :] = s * (1.0 + v * (1.0 - s))
        v = node_pre[rows, :]
        s = sigmoid(v)
        node_pre[rows, :] = s * (1.0 + v * (1.0 - s))

    summed_act_t[...] = jnp.transpose(summed_act[...].astype(F32)).astype(BF16)

    whole(pred_in.at[pl.ds(1, n_ens - 1)], 1).wait_recv()
    weight_row = var_ref[...]

    @pl.loop(0, chunk // 8)
    def _(i):
        rows = pl.ds(pl.multiple_of(i * 8, 8), 8)
        goal = target[pl.ds(pl.multiple_of(ens * chunk + i * 8, 8), 8), :]
        mine = [pred_in[m, rows, :] for m in range(n_ens)]
        pairwise = [jnp.zeros_like(goal) for _ in range(n_ens)]
        for a in range(n_ens):
            for b in range(a + 1, n_ens):
                t = mine[a] - mine[b]
                g = t * lax.rsqrt(t * t + SOFT)
                pairwise[a] += g
                pairwise[b] -= g
        for m in range(n_ens):
            t = mine[m] - goal
            g = t * lax.rsqrt(t * t + SOFT)
            grad_wide[m, rows, :] = weight_row * (g - pairwise[m] * (1.0 / (n_ens - 1.0)))

    grad_out[...] = grad_wide[...].astype(BF16)
    grad_in[0] = grad_out[0]
    exchange(grad_out, grad_in, 2, "ens", ens, n_ens)
    whole(grad_in.at[pl.ds(1, n_ens - 1)], 2).wait_recv()

    @pl.loop(0, n_ens)
    def _(q):
        pred_grad[lax.rem(ens + q, n_ens)] = grad_in[q]

    hidden_grad = (
        dot(pred_grad[...].reshape(points, LANES), w_out[...]) * node_pre[...]
    ).astype(BF16)
    edge_grad[...] = dot_t(hidden_grad, w_node[...]).astype(BF16)

    theirs = pl.ds(pl.multiple_of((1 - core) * half, half), half)
    ours = pl.ds(pl.multiple_of(core * half, half), half)
    pair_out[...] = dot(summed_act_t[theirs, :], edge_grad[...]).astype(BF16)
    pair = pltpu.make_async_remote_copy(
        src_ref=pair_out,
        dst_ref=pair_in,
        send_sem=send_sem.at[3],
        recv_sem=recv_sem.at[3],
        device_id={"ens": ens + 1 - 2 * core},
        device_id_type=MESH,
    )
    pair.start()
    back[...] = dot_t(edge_grad[...], w_msg[...])
    own_half[...] = dot(summed_act_t[ours, :], edge_grad[...])
    pair.wait_recv()
    z_out[...] = (own_half[...] + pair_in[...].astype(F32)).astype(BF16).reshape(z_out.shape)
    z_in[0] = z_out[z]

    @pl.loop(1, n_z)
    def _(q):
        to = lax.rem(z + q, n_z)
        pltpu.make_async_remote_copy(
            src_ref=z_out.at[to],
            dst_ref=z_in.at[n_z - q],
            send_sem=send_sem.at[4],
            recv_sem=recv_sem.at[4],
            device_id={"ens": 2 * to + core},
            device_id_type=MESH,
        ).start()

    @pl.loop(0, points // step)
    def _(i):
        rows = pl.ds(pl.multiple_of(i * step, step), step)
        b = back[rows, :]
        for k in range(per_point):
            pre_grad[k, rows, :] = (b * pre[k, rows, :]).astype(BF16)

    slot_grad = dot(one_hot_t[...], pre_grad[...].reshape(per_point * points, features))
    blocks = to_blocks(slot_grad, n_sp).astype(BF16)
    rows_out[...] = blocks
    rows_in[0] = blocks[0]
    exchange(rows_out, rows_in, 5, "space", sp, n_sp)

    whole(z_in.at[pl.ds(1, n_z - 1)], 4).wait_recv()
    part = jnp.sum(z_in[...].astype(F32), axis=0)
    part_out[...] = part.astype(BF16).reshape(part_out.shape)
    index = core * n_z + z
    for i in range(per_block):
        to = index * per_block + i

        @pl.when(to != sp)
        def _():
            pltpu.make_async_remote_copy(
                src_ref=part_out.at[i],
                dst_ref=part_in.at[lax.rem(sp - to + n_sp, n_sp)],
                send_sem=send_sem.at[6],
                recv_sem=recv_sem.at[6],
                device_id={"space": to},
                device_id_type=MESH,
            ).start()

        @pl.when(to == sp)
        def _():
            part_in[0] = part_out[i]

    whole(rows_in.at[pl.ds(1, n_sp - 1)], 5).wait_recv()
    back_rows = from_blocks(rows_in[...].astype(F32)).astype(BF16)
    row_grads = dot(pick_t[...], back_rows)
    high = row_grads.astype(BF16)
    low = (row_grads - high.astype(F32)).astype(BF16)
    mesh_ref[...] = dot_t(high, w_send[...]) + dot_t(low, w_send[...])

    owner = lax.div(sp, per_block) == index

    @pl.when(owner)
    def _():
        whole(part_in.at[pl.ds(1, n_sp - 1)], 6).wait_recv()
        total = jnp.sum(part_in[...].astype(F32), axis=0)
        weight_ref[...] = total * scale
        total_out[...] = total.astype(BF16)

        @pl.loop(1, n_ens)
        def _(q):
            pltpu.make_async_remote_copy(
                src_ref=total_out,
                dst_ref=total_in,
                send_sem=send_sem.at[7],
                recv_sem=recv_sem.at[7],
                device_id={"ens": lax.rem(ens + q, n_ens)},
                device_id_type=MESH,
            ).start()

        @pl.loop(1, n_ens)
        def _(q):
            whole(total_out, 7).wait_send()

    @pl.when(jnp.logical_not(owner))
    def _():
        whole(total_in, 7).wait_recv()
        weight_ref[...] = total_in[...].astype(F32) * scale

    for i in range(per_block):

        @pl.when(index * per_block + i != sp)
        def _():
            whole(part_out.at[i], 6).wait_send()

    whole(out_rows.at[pl.ds(1, n_sp - 1)], 0).wait_send()
    whole(pred_in.at[pl.ds(1, n_ens - 1)], 1).wait_send()
    whole(grad_out.at[pl.ds(1, n_ens - 1)], 2).wait_send()
    pair.wait_send()
    whole(z_in.at[pl.ds(1, n_z - 1)], 4).wait_send()
    whole(rows_out.at[pl.ds(1, n_sp - 1)], 5).wait_send()


def body(
    n_ens,
    n_sp,
    mesh_latent,
    grid_embed,
    w_send,
    w_recv,
    w_msg,
    w_node,
    w_out,
    target,
    var_weight,
    send_rows,
    edge_slot,
    edge_count,
):
    local_rows, features = mesh_latent.shape[1:]
    points, per_point = edge_slot.shape
    variables = target.shape[1]
    cap = send_rows.shape[2]
    slots = n_sp * cap
    chunk = points // n_ens
    half = features // 2
    n_z = n_ens // 2
    out_block = features // n_sp
    per_block = n_sp // n_ens
    total = n_ens * points * n_sp * per_point
    hbm = pl.BlockSpec(memory_space=pl.ANY)
    vmem = pl.BlockSpec(memory_space=pltpu.VMEM)
    square = (features, features)
    rows_blocks = (n_sp, 2 * cap, half)
    scratch = [
        pltpu.VMEM((local_rows, features), BF16),
        pltpu.VMEM((points, features), BF16),
        pltpu.VMEM(square, BF16),
        pltpu.VMEM(square, BF16),
        pltpu.VMEM(square, BF16),
        pltpu.VMEM(square, BF16),
        pltpu.VMEM((variables, features), BF16),
        pltpu.VMEM((variables, points), F32),
        pltpu.VMEM((LANES, features), F32),
        pltpu.VMEM((LANES, features), BF16),
        pltpu.VMEM((LANES, points), F32),
        pltpu.VMEM((points, LANES), F32),
        pltpu.VMEM((LANES, points), F32),
        pltpu.VMEM((points, LANES), F32),
        pltpu.VMEM((slots, local_rows), BF16),
        pltpu.VMEM((local_rows, slots), BF16),
        pltpu.VMEM(rows_blocks, BF16),
        pltpu.VMEM(rows_blocks, BF16),
        pltpu.VMEM((slots, features), BF16),
        pltpu.VMEM((points, features), F32),
        pltpu.VMEM((per_point, points, slots), BF16),
        pltpu.VMEM((slots, per_point * points), BF16),
        pltpu.VMEM((per_point, points, features), F32),
        pltpu.VMEM((per_point, points, LANES), F32),
        pltpu.VMEM((points, features), BF16),
        pltpu.VMEM((features, points), BF16),
        pltpu.VMEM((points, features), F32),
        pltpu.VMEM((n_ens, chunk, LANES), F32),
        pltpu.VMEM((n_ens, chunk, LANES), F32),
        pltpu.VMEM((n_ens, chunk, LANES), F32),
        pltpu.VMEM((n_ens, chunk, LANES), BF16),
        pltpu.VMEM((n_ens, chunk, LANES), BF16),
        pltpu.VMEM((n_ens, chunk, LANES), BF16),
        pltpu.VMEM((points, features), BF16),
        pltpu.VMEM((points, features), F32),
        pltpu.VMEM((per_point, points, features), BF16),
        pltpu.VMEM((half, features), F32),
        pltpu.VMEM((half, features), BF16),
        pltpu.VMEM((half, features), BF16),
        pltpu.VMEM((n_z, features // n_ens, features), BF16),
        pltpu.VMEM((n_z, features // n_ens, features), BF16),
        pltpu.VMEM((per_block, out_block, features), BF16),
        pltpu.VMEM((n_sp, out_block, features), BF16),
        pltpu.VMEM((out_block, features), BF16),
        pltpu.VMEM((out_block, features), BF16),
        pltpu.VMEM(rows_blocks, BF16),
        pltpu.VMEM(rows_blocks, BF16),
        pltpu.SemaphoreType.DMA((8,)),
        pltpu.SemaphoreType.DMA((8,)),
        pltpu.SemaphoreType.DMA((8,)),
    ]
    mesh_grad, weight_grad = pl.pallas_call(
        functools.partial(kernel, n_ens, n_sp, 1.0 / math.sqrt(total)),
        out_shape=(
            jax.ShapeDtypeStruct((local_rows, features), F32),
            jax.ShapeDtypeStruct((out_block, features), F32),
        ),
        in_specs=[hbm] * 8 + [vmem] * 4,
        out_specs=(vmem, vmem),
        scratch_shapes=scratch,
        compiler_params=pltpu.CompilerParams(
            collective_id=0, has_side_effects=True, vmem_limit_bytes=60 * 1024 * 1024
        ),
    )(
        mesh_latent[0],
        grid_embed,
        w_send,
        w_recv,
        w_msg,
        w_node,
        w_out.T,
        target.T,
        jnp.pad(var_weight, (0, LANES - variables)).reshape(1, LANES),
        jnp.swapaxes(send_rows[0], 0, 1),
        edge_slot.T,
        edge_count.reshape(1, points),
    )
    return (mesh_grad[None], weight_grad)


def solution(mesh):
    in_specs = (
        P("ens", "space", None),
        P("space", None),
        P(),
        P(),
        P(),
        P(),
        P(),
        P("space", None),
        P(),
        P("space", None, None),
        P("space", None),
        P("space"),
    )
    out_specs = (P("ens", "space", None), P("space", None))
    return jax.shard_map(
        functools.partial(body, mesh.shape["ens"], mesh.shape["space"]),
        mesh=mesh,
        in_specs=in_specs,
        out_specs=out_specs,
        check_vma=False,
    )
```

```python
import functools
import math

import jax
import jax.numpy as jnp
from jax import lax
from jax.experimental import pallas as pl
from jax.experimental.pallas import tpu as pltpu
from jax.sharding import PartitionSpec as P

MESH = pl.DeviceIdType.MESH
F32 = jnp.float32
BF16 = jnp.bfloat16
SOFT = 0.09
LANES = 128
ALONG_X = 4
PARTS = 2


def sigmoid(v):
    return 0.5 * jnp.tanh(0.5 * v) + 0.5


def dot(a, b):
    return jnp.dot(a, b, preferred_element_type=F32)


def dot_t(a, b):
    return lax.dot_general(a, b, (((1,), (1,)), ((), ())), preferred_element_type=F32)


def to_blocks(rows, n):
    c, f = rows.shape[0] // n, rows.shape[1]
    split = rows.reshape(n, c, f)
    return jnp.concatenate([split[:, :, : f // 2], split[:, :, f // 2 :]], axis=1)


def from_blocks(blocks):
    n, c2, f2 = blocks.shape
    c = c2 // 2
    left = blocks[:, :c, :].reshape(n * c, f2)
    right = blocks[:, c:, :].reshape(n * c, f2)
    return jnp.concatenate([left, right], axis=1)


def wrap(i, n):
    return jnp.where(i < 0, i + n, jnp.where(i >= n, i - n, i))


def from_far(t, n):
    return n // 2 + (1 - 2 * lax.rem(t, 2)) * lax.div(t + 1, 2)


def kernel(
    n_ens,
    n_sp,
    scale,
    lat_h,
    emb_h,
    w_send_h,
    w_recv_h,
    w_msg_h,
    w_node_h,
    w_out_h,
    target_h,
    var_h,
    rows_h,
    slot_h,
    count_h,
    rows_grad_ref,
    w_send_ref,
    weight_ref,
    lat,
    rows_ref,
    emb,
    w_recv,
    w_msg,
    w_node,
    w_out_raw,
    target_raw,
    var_ref,
    slot_ref,
    count_ref,
    wide,
    w_out,
    target_wide,
    target,
    var_wide,
    small,
    columns,
    pick,
    pick_t,
    out_rows,
    in_rows,
    slot_proj,
    grid_proj,
    one_hot,
    one_hot_t,
    pre,
    live,
    summed_act,
    summed_act_t,
    node_pre,
    pred,
    pred_in,
    grad_wide,
    grad_out,
    grad_in,
    pred_grad,
    edge_grad,
    back,
    pre_grad,
    slot_grad,
    halves,
    pair_out,
    pair_in,
    sum_out,
    sum_in,
    total_out,
    total_in,
    rows_out,
    rows_in,
    load_sem,
    send_sem,
    recv_sem,
):
    ens = lax.axis_index("ens")
    sp = lax.axis_index("space")
    core = lax.rem(ens, 2)
    n_x = ALONG_X
    n_y = n_sp // n_x
    y = lax.div(sp, n_x)
    x = lax.rem(sp, n_x)
    points, features = emb.shape
    per_point = slot_ref.shape[0]
    cap = rows_ref.shape[0]
    slots = n_sp * cap
    part_points = points // PARTS
    half = features // 2
    w_send = w_send_ref

    loads = [
        pltpu.make_async_copy(src, dst, load_sem.at[i])
        for i, (src, dst) in enumerate(
            [
                (rows_h, rows_ref),
                (lat_h, lat),
                (emb_h, emb),
                (w_recv_h, w_recv),
                (slot_h, slot_ref),
                (count_h, count_ref),
                (w_send_h, w_send),
                (w_msg_h, w_msg),
                (w_node_h, w_node),
                (w_out_h, w_out_raw),
                (target_h, target_raw),
                (var_h, var_ref),
            ]
        )
    ]
    for load in loads:
        load.start()

    def space_peer(t):
        dy = from_far(lax.div(t, n_x), n_y)
        dx = from_far(lax.rem(t, n_x), n_x)
        to = lax.rem(y + dy, n_y) * n_x + lax.rem(x + dx, n_x)
        back_place = lax.rem(n_y - dy, n_y) * n_x + lax.rem(n_x - dx, n_x)
        return to, dy * n_x + dx, back_place

    barrier = pltpu.get_barrier_semaphore()

    @pl.loop(0, n_sp - 1)
    def _(t):
        to, _, _ = space_peer(t)
        pl.semaphore_signal(barrier, inc=1, device_id={"space": to}, device_id_type=MESH)

    @pl.loop(0, n_ens - 1)
    def _(t):
        to = lax.rem(ens + from_far(t, n_ens), n_ens)
        pl.semaphore_signal(barrier, inc=1, device_id={"ens": to}, device_id_type=MESH)

    def remote(src, dst, which, to):
        return pltpu.make_async_remote_copy(
            src_ref=src,
            dst_ref=dst,
            send_sem=send_sem.at[which],
            recv_sem=recv_sem.at[which],
            device_id=to,
            device_id_type=MESH,
        )

    def whole(ref, which):
        return remote(ref, ref, which, {"ens": ens})

    loads[0].wait()
    tiled = jnp.broadcast_to(
        rows_ref[...].astype(F32)[None], (n_sp, cap, n_sp)
    ).reshape(slots, n_sp)
    place = lax.broadcasted_iota(jnp.int32, (slots, n_sp), 0) // cap
    receiver = wrap(place // n_x + y, n_y) * n_x + wrap(place % n_x + x, n_x)
    lane = lax.broadcasted_iota(jnp.int32, (slots, n_sp), 1)
    wanted = jnp.sum(jnp.where(lane == receiver, tiled, 0.0), axis=1, keepdims=True)
    local_rows = lat.shape[0]
    pick_wide = jnp.where(
        lax.broadcasted_iota(jnp.int32, (slots, local_rows), 1).astype(F32) == wanted, 1.0, 0.0
    )
    pick[...] = pick_wide.astype(BF16)
    loads[1].wait()
    blocks = to_blocks(dot(pick[...], lat[...]), n_sp).astype(BF16)
    out_rows[...] = blocks
    in_rows[0] = blocks[0]
    pl.semaphore_wait(barrier, n_sp + n_ens - 2)

    def space_exchange(src, dst, which):
        @pl.loop(0, n_sp - 1)
        def _(t):
            to, place, back_place = space_peer(t)
            remote(src.at[place], dst.at[back_place], which, {"space": to}).start()

    space_exchange(out_rows, in_rows, 0)

    loads[2].wait()
    loads[3].wait()
    grid_proj[...] = dot(emb[...], w_recv[...])
    pick_t[...] = jnp.transpose(pick_wide).astype(BF16)
    loads[4].wait()
    loads[5].wait()
    sender = slot_ref[...] // cap
    slot = (
        wrap(sender // n_x - y, n_y) * n_x + wrap(sender % n_x - x, n_x)
    ) * cap + slot_ref[...] % cap
    is_live = lax.broadcasted_iota(jnp.int32, slot.shape, 0) < count_ref[...]
    small[...] = jnp.zeros_like(small)
    small[0:per_point, :] = slot.astype(F32)
    small[per_point : 2 * per_point, :] = jnp.where(is_live, 1.0, 0.0)
    columns[...] = jnp.transpose(small[...])
    slot = jnp.where(is_live, slot, -1)
    slot_index = lax.broadcasted_iota(jnp.int32, (slots, part_points), 0)
    lane_index = lax.broadcasted_iota(jnp.int32, (points, slots), 1).astype(F32)
    for k in range(per_point):
        one_hot[k] = jnp.where(lane_index == columns[:, k : k + 1], 1.0, 0.0).astype(BF16)
        for h in range(PARTS):
            one_hot_t[h, :, k * part_points : (k + 1) * part_points] = jnp.where(
                slot_index == slot[k : k + 1, h * part_points : (h + 1) * part_points], 1.0, 0.0
            ).astype(BF16)
        live[k] = jnp.broadcast_to(
            columns[:, per_point + k : per_point + k + 1], (points, LANES)
        )
    loads[9].wait()
    variables = w_out_raw.shape[0]
    wide[...] = jnp.zeros_like(wide)
    wide[0:variables, :] = w_out_raw[...].astype(F32)
    w_out[...] = wide[...].astype(BF16)
    loads[10].wait()
    target_wide[...] = jnp.zeros_like(target_wide)
    target_wide[0:variables, :] = target_raw[...]
    target[...] = jnp.transpose(target_wide[...])
    loads[11].wait()
    var_wide[...] = jnp.zeros_like(var_wide)
    var_wide[0:1, 0:variables] = var_ref[...]
    loads[6].wait()
    loads[7].wait()
    loads[8].wait()

    step = 16

    def rows_of(h, i):
        return pl.ds(pl.multiple_of(h * part_points + i * step, step), step)

    def spread(k, rows):
        return jnp.concatenate([live[k, rows, :]] * (features // LANES), axis=1)

    def forward(h):
        span = pl.ds(h * part_points, part_points)
        for k in range(per_point):
            pre[k, span, :] = dot(one_hot[k, span, :], slot_proj[...])

        @pl.loop(0, part_points // step)
        def _(i):
            rows = rows_of(h, i)
            base = grid_proj[rows, :]
            total = jnp.zeros((step, features), F32)
            for k in range(per_point):
                v = pre[k, rows, :] + base
                total += v * sigmoid(v) * spread(k, rows)
            summed_act[rows, :] = total.astype(BF16)

        node_in = (
            dot(summed_act[span, :], w_msg[...]) + emb[span, :].astype(F32)
        ).astype(BF16)
        v = dot(node_in, w_node[...])
        node_pre[span, :] = v
        hidden = (v * sigmoid(v)).astype(BF16)
        pred[h] = dot_t(hidden, w_out[...]).reshape(pred.shape[1:])

        pred_in[h, 0] = pred[h, ens]

        @pl.loop(0, n_ens - 1)
        def _(t):
            q = from_far(t, n_ens)
            to = lax.rem(ens + q, n_ens)
            remote(pred.at[h, to], pred_in.at[h, n_ens - q], 1 + h, {"ens": to}).start()

    def slopes(h):
        @pl.loop(0, part_points // step)
        def _(i):
            rows = rows_of(h, i)
            base = grid_proj[rows, :]
            for k in range(per_point):
                v = pre[k, rows, :] + base
                s = sigmoid(v)
                pre[k, rows, :] = s * (1.0 + v * (1.0 - s))
            v = node_pre[rows, :]
            s = sigmoid(v)
            node_pre[rows, :] = s * (1.0 + v * (1.0 - s))

    def scores(h):
        whole(pred_in.at[h, pl.ds(1, n_ens - 1)], 1 + h).wait_recv()
        share = part_points // n_ens

        @pl.loop(0, share // 8)
        def _(i):
            rows = pl.ds(pl.multiple_of(i * 8, 8), 8)
            goal = target[
                pl.ds(pl.multiple_of(h * part_points + ens * share + i * 8, 8), 8), :
            ]
            mine = [pred_in[h, m, rows, :] for m in range(n_ens)]
            pairwise = [jnp.zeros_like(goal) for _ in range(n_ens)]
            for a in range(n_ens):
                for b in range(a + 1, n_ens):
                    t = mine[a] - mine[b]
                    g = t * lax.rsqrt(t * t + SOFT)
                    pairwise[a] += g
                    pairwise[b] -= g
            weight_row = var_wide[0:1, :]
            for m in range(n_ens):
                t = mine[m] - goal
                g = t * lax.rsqrt(t * t + SOFT)
                grad_wide[m, rows, :] = weight_row * (g - pairwise[m] * (1.0 / (n_ens - 1.0)))

        grad_out[h] = grad_wide[...].astype(BF16)
        grad_in[h, 0] = grad_out[h, 0]

        @pl.loop(0, n_ens - 1)
        def _(t):
            q = from_far(t, n_ens)
            to = lax.rem(ens + q, n_ens)
            remote(
                grad_out.at[h, q], grad_in.at[h, n_ens - q], 1 + PARTS + h, {"ens": to}
            ).start()

    def edge_backward(h):
        whole(grad_in.at[h, pl.ds(1, n_ens - 1)], 1 + PARTS + h).wait_recv()

        @pl.loop(0, n_ens)
        def _(q):
            pred_grad[h, lax.rem(ens + q, n_ens)] = grad_in[h, q]

        span = pl.ds(h * part_points, part_points)
        hidden_grad = (
            dot(pred_grad[h].reshape(part_points, LANES), w_out[...]) * node_pre[span, :]
        ).astype(BF16)
        edge_grad[h] = dot_t(hidden_grad, w_node[...]).astype(BF16)

    def weight_half(which, h):
        return dot(summed_act_t[which, :, h * part_points : (h + 1) * part_points], edge_grad[h])

    def slot_backward(h):
        @pl.loop(0, part_points // step)
        def _(i):
            rows = rows_of(h, i)
            b = back[pl.ds(pl.multiple_of(i * step, step), step), :]
            for k in range(per_point):
                pre_grad[
                    pl.ds(pl.multiple_of(k * part_points + i * step, step), step), :
                ] = (b * pre[k, rows, :]).astype(BF16)

        return dot(one_hot_t[h], pre_grad[...])

    whole(in_rows.at[pl.ds(1, n_sp - 1)], 0).wait_recv()
    arrived = from_blocks(in_rows[...].astype(F32)).astype(BF16)
    slot_proj[...] = dot(arrived, w_send[...]).astype(BF16)
    for h in range(PARTS):
        forward(h)

    for h in range(PARTS):
        slopes(h)
    turned = jnp.transpose(summed_act[...].astype(F32)).reshape(n_sp, 2, features // n_sp // 2, points)
    for c in range(2):
        summed_act_t[c] = turned[:, c].reshape(half, points).astype(BF16)

    for h in range(PARTS):
        scores(h)

    theirs, ours = 1 - core, core
    for h in range(PARTS - 1):
        edge_backward(h)
        back[...] = dot_t(edge_grad[h], w_msg[...])
        for i, which in enumerate((theirs, ours)):
            term = weight_half(which, h)
            halves[i] = term if h == 0 else halves[i] + term
        term = slot_backward(h)
        slot_grad[...] = term if h == 0 else slot_grad[...] + term

    last = PARTS - 1
    edge_backward(last)
    pair_out[...] = (halves[0] + weight_half(theirs, last)).astype(BF16)
    pair = remote(pair_out, pair_in, 7, {"ens": ens + 1 - 2 * core})
    pair.start()
    back[...] = dot_t(edge_grad[last], w_msg[...])
    own = halves[1] + weight_half(ours, last)
    halves[1] = own
    pair.wait_recv()
    blocks = to_blocks(halves[1] + pair_in[...].astype(F32), n_sp).astype(BF16)
    sum_out[...] = blocks
    sum_in[0] = sum_out[sp]

    @pl.loop(0, n_sp - 1)
    def _(t):
        to, _, back_place = space_peer(t)
        remote(sum_out.at[to], sum_in.at[back_place], 5, {"space": to}).start()

    blocks = to_blocks(slot_grad[...] + slot_backward(last), n_sp).astype(BF16)
    rows_out[...] = blocks
    rows_in[0] = blocks[0]
    space_exchange(rows_out, rows_in, 6)

    whole(sum_in.at[pl.ds(1, n_sp - 1)], 5).wait_recv()
    total_out[...] = jnp.sum(sum_in[...].astype(F32), axis=0).astype(BF16)
    total_in[0] = total_out[...]

    @pl.loop(0, n_ens - 1)
    def _(t):
        q = from_far(t, n_ens)
        to = lax.rem(ens + q, n_ens)
        remote(total_out, total_in.at[n_ens - q], 8, {"ens": to}).start()

    whole(rows_in.at[pl.ds(1, n_sp - 1)], 6).wait_recv()
    back_rows = from_blocks(rows_in[...].astype(F32)).astype(BF16)
    rows_grad_ref[...] = dot(pick_t[...], back_rows)

    whole(total_in.at[pl.ds(1, n_ens - 1)], 8).wait_recv()
    same = total_in[0].astype(F32)
    other = total_in[1].astype(F32)
    for q in range(2, n_ens, 2):
        same += total_in[q].astype(F32)
        other += total_in[q + 1].astype(F32)
    first = jnp.where(core == 0, same, other)
    second = jnp.where(core == 0, other, same)
    weight_ref[...] = scale * jnp.concatenate(
        [from_blocks(first[None]), from_blocks(second[None])], axis=0
    )

    whole(out_rows.at[pl.ds(1, n_sp - 1)], 0).wait_send()
    for h in range(PARTS):
        whole(pred_in.at[h, pl.ds(1, n_ens - 1)], 1 + h).wait_send()
        whole(grad_out.at[h, pl.ds(1, n_ens - 1)], 1 + PARTS + h).wait_send()
    pair.wait_send()
    whole(sum_in.at[pl.ds(1, n_sp - 1)], 5).wait_send()
    whole(rows_out.at[pl.ds(1, n_sp - 1)], 6).wait_send()
    whole(total_in.at[pl.ds(1, n_ens - 1)], 8).wait_send()


def last_kernel(rows_ref, w_send_ref, weight_in, mesh_ref, weight_ref):
    rows = rows_ref[...]
    high = rows.astype(BF16)
    low = (rows - high.astype(F32)).astype(BF16)
    mesh_ref[...] = dot_t(high, w_send_ref[...]) + dot_t(low, w_send_ref[...])
    weight_ref[...] = weight_in[...]


def body(
    n_ens,
    n_sp,
    mesh_latent,
    grid_embed,
    w_send,
    w_recv,
    w_msg,
    w_node,
    w_out,
    target,
    var_weight,
    send_rows,
    edge_slot,
    edge_count,
):
    local_rows, features = mesh_latent.shape[1:]
    points, per_point = edge_slot.shape
    variables = target.shape[1]
    cap = send_rows.shape[2]
    slots = n_sp * cap
    part_points = points // PARTS
    share = part_points // n_ens
    half = features // 2
    out_block = features // n_sp
    total = n_ens * points * n_sp * per_point
    hbm = pl.BlockSpec(memory_space=pltpu.HBM)
    vmem = pl.BlockSpec(memory_space=pltpu.VMEM)
    square = (features, features)
    rows_blocks = (n_sp, 2 * cap, half)
    shares = (PARTS, n_ens, share, LANES)
    scratch = [
        pltpu.VMEM((local_rows, features), BF16),
        pltpu.VMEM((cap, n_sp), jnp.int32),
        pltpu.VMEM((points, features), BF16),
        pltpu.VMEM(square, BF16),
        pltpu.VMEM(square, BF16),
        pltpu.VMEM(square, BF16),
        pltpu.VMEM((variables, features), BF16),
        pltpu.VMEM((variables, points), F32),
        pltpu.VMEM((1, variables), F32),
        pltpu.VMEM((per_point, points), jnp.int32),
        pltpu.VMEM((1, points), jnp.int32),
        pltpu.VMEM((LANES, features), F32),
        pltpu.VMEM((LANES, features), BF16),
        pltpu.VMEM((LANES, points), F32),
        pltpu.VMEM((points, LANES), F32),
        pltpu.VMEM((8, LANES), F32),
        pltpu.VMEM((LANES, points), F32),
        pltpu.VMEM((points, LANES), F32),
        pltpu.VMEM((slots, local_rows), BF16),
        pltpu.VMEM((local_rows, slots), BF16),
        pltpu.VMEM(rows_blocks, BF16),
        pltpu.VMEM(rows_blocks, BF16),
        pltpu.VMEM((slots, features), BF16),
        pltpu.VMEM((points, features), F32),
        pltpu.VMEM((per_point, points, slots), BF16),
        pltpu.VMEM((PARTS, slots, per_point * part_points), BF16),
        pltpu.VMEM((per_point, points, features), F32),
        pltpu.VMEM((per_point, points, LANES), F32),
        pltpu.VMEM((points, features), BF16),
        pltpu.VMEM((2, half, points), BF16),
        pltpu.VMEM((points, features), F32),
        pltpu.VMEM(shares, F32),
        pltpu.VMEM(shares, F32),
        pltpu.VMEM(shares[1:], F32),
        pltpu.VMEM(shares, BF16),
        pltpu.VMEM(shares, BF16),
        pltpu.VMEM(shares, BF16),
        pltpu.VMEM((PARTS, part_points, features), BF16),
        pltpu.VMEM((part_points, features), F32),
        pltpu.VMEM((per_point * part_points, features), BF16),
        pltpu.VMEM((slots, features), F32),
        pltpu.VMEM((2, half, features), F32),
        pltpu.VMEM((half, features), BF16),
        pltpu.VMEM((half, features), BF16),
        pltpu.VMEM((n_sp, out_block, half), BF16),
        pltpu.VMEM((n_sp, out_block, half), BF16),
        pltpu.VMEM((out_block, half), BF16),
        pltpu.VMEM((n_ens, out_block, half), BF16),
        pltpu.VMEM(rows_blocks, BF16),
        pltpu.VMEM(rows_blocks, BF16),
        pltpu.SemaphoreType.DMA((12,)),
        pltpu.SemaphoreType.DMA((9,)),
        pltpu.SemaphoreType.DMA((9,)),
    ]
    row_grads, w_send_near, weight_grad = pl.pallas_call(
        functools.partial(kernel, n_ens, n_sp, 1.0 / math.sqrt(total)),
        out_shape=(
            jax.ShapeDtypeStruct((local_rows, features), F32),
            jax.ShapeDtypeStruct(square, BF16),
            jax.ShapeDtypeStruct((out_block, features), F32),
        ),
        in_specs=[hbm] * 12,
        out_specs=(vmem, vmem, vmem),
        scratch_shapes=scratch,
        compiler_params=pltpu.CompilerParams(
            collective_id=0, has_side_effects=True, vmem_limit_bytes=48 * 1024 * 1024
        ),
    )(
        *(
            pltpu.with_memory_space_constraint(array, pltpu.HBM)
            for array in (
                mesh_latent[0],
                grid_embed,
                w_send,
                w_recv,
                w_msg,
                w_node,
                w_out.T,
                target.T,
                var_weight.reshape(1, variables),
                jnp.swapaxes(send_rows[0], 0, 1),
                edge_slot.T,
                edge_count.reshape(1, points),
            )
        )
    )
    mesh_grad, weight_grad = pl.pallas_call(
        last_kernel,
        out_shape=(
            jax.ShapeDtypeStruct((local_rows, features), F32),
            jax.ShapeDtypeStruct((out_block, features), F32),
        ),
        in_specs=[vmem] * 3,
        out_specs=(vmem, vmem),
    )(row_grads, w_send_near, weight_grad)
    return (mesh_grad[None], weight_grad)


def solution(mesh):
    in_specs = (
        P("ens", "space", None),
        P("space", None),
        P(),
        P(),
        P(),
        P(),
        P(),
        P("space", None),
        P(),
        P("space", None, None),
        P("space", None),
        P("space"),
    )
    out_specs = (P("ens", "space", None), P("space", None))
    return jax.shard_map(
        functools.partial(body, mesh.shape["ens"], mesh.shape["space"]),
        mesh=mesh,
        in_specs=in_specs,
        out_specs=out_specs,
        check_vma=False,
    )
```

```python
import functools
import math

import jax
import jax.numpy as jnp
from jax import lax
from jax.experimental import pallas as pl
from jax.experimental.pallas import tpu as pltpu
from jax.sharding import PartitionSpec as P

MESH = pl.DeviceIdType.MESH
F32 = jnp.float32
BF16 = jnp.bfloat16
SOFT = 0.09
LANES = 128
ALONG_X = 4
PARTS = 2


def silu(u):
    return u * jnp.tanh(u) + u


def twice_slope(u):
    t = jnp.tanh(u)
    return 1.0 + t + u * (1.0 - t * t)


def dot(a, b):
    return jnp.dot(a, b, preferred_element_type=F32)


def dot_t(a, b):
    return lax.dot_general(a, b, (((1,), (1,)), ((), ())), preferred_element_type=F32)


def to_blocks(rows, n):
    c, f = rows.shape[0] // n, rows.shape[1]
    split = rows.reshape(n, c, f)
    return jnp.concatenate([split[:, :, : f // 2], split[:, :, f // 2 :]], axis=1)


def from_blocks(blocks):
    n, c2, f2 = blocks.shape
    c = c2 // 2
    left = blocks[:, :c, :].reshape(n * c, f2)
    right = blocks[:, c:, :].reshape(n * c, f2)
    return jnp.concatenate([left, right], axis=1)


def wrap(i, n):
    return jnp.where(i < 0, i + n, jnp.where(i >= n, i - n, i))


def from_far(t, n):
    return n // 2 + (1 - 2 * lax.rem(t, 2)) * lax.div(t + 1, 2)


def kernel(
    n_ens,
    n_sp,
    scale,
    lat_h,
    emb_h,
    w_send_h,
    w_recv_h,
    w_msg_h,
    w_node_h,
    w_out_h,
    target_h,
    var_h,
    rows_h,
    slot_h,
    count_h,
    mesh_ref,
    weight_ref,
    lat,
    rows_ref,
    emb,
    w_send,
    w_recv,
    w_msg,
    w_node,
    w_out_raw,
    target_raw,
    var_ref,
    slot_ref,
    count_ref,
    wide,
    w_out,
    target_wide,
    target,
    var_wide,
    small,
    columns,
    pick,
    pick_t,
    out_rows,
    in_rows,
    slot_proj,
    grid_proj,
    one_hot,
    one_hot_t,
    pre,
    live,
    summed_act,
    summed_act_t,
    node_pre,
    pred,
    pred_in,
    pred_wide,
    grad_wide,
    grad_out,
    grad_in,
    pred_grad,
    edge_grad,
    back,
    pre_grad,
    slot_grad,
    halves,
    pair_out,
    pair_in,
    sum_out,
    sum_in,
    total_out,
    total_in,
    rows_out,
    rows_in,
    load_sem,
    send_sem,
    recv_sem,
):
    ens = lax.axis_index("ens")
    sp = lax.axis_index("space")
    core = lax.rem(ens, 2)
    n_x = ALONG_X
    n_y = n_sp // n_x
    y = lax.div(sp, n_x)
    x = lax.rem(sp, n_x)
    points, features = emb.shape
    per_point = slot_ref.shape[0]
    cap = rows_ref.shape[0]
    slots = n_sp * cap
    part_points = points // PARTS
    half = features // 2

    def space_peer(t):
        dy = from_far(lax.div(t, n_x), n_y)
        dx = from_far(lax.rem(t, n_x), n_x)
        to = lax.rem(y + dy, n_y) * n_x + lax.rem(x + dx, n_x)
        back_place = lax.rem(n_y - dy, n_y) * n_x + lax.rem(n_x - dx, n_x)
        return to, dy * n_x + dx, back_place

    barrier = pltpu.get_barrier_semaphore()

    @pl.loop(0, n_sp - 1)
    def _(t):
        to, _, _ = space_peer(t)
        pl.semaphore_signal(barrier, inc=1, device_id={"space": to}, device_id_type=MESH)

    @pl.loop(0, n_ens - 1)
    def _(t):
        to = lax.rem(ens + from_far(t, n_ens), n_ens)
        pl.semaphore_signal(barrier, inc=1, device_id={"ens": to}, device_id_type=MESH)

    loads = [
        pltpu.make_async_copy(src, dst, load_sem.at[i])
        for i, (src, dst) in enumerate(
            [
                (rows_h, rows_ref),
                (lat_h, lat),
                (emb_h, emb),
                (w_recv_h, w_recv),
                (slot_h, slot_ref),
                (count_h, count_ref),
                (w_send_h, w_send),
                (w_msg_h, w_msg),
                (w_node_h, w_node),
                (w_out_h, w_out_raw),
                (target_h, target_raw),
                (var_h, var_ref),
            ]
        )
    ]
    for load in loads:
        load.start()

    def remote(src, dst, which, to):
        return pltpu.make_async_remote_copy(
            src_ref=src,
            dst_ref=dst,
            send_sem=send_sem.at[which],
            recv_sem=recv_sem.at[which],
            device_id=to,
            device_id_type=MESH,
        )

    def whole(ref, which):
        return remote(ref, ref, which, {"ens": ens})

    loads[0].wait()
    tiled = jnp.broadcast_to(
        rows_ref[...].astype(F32)[None], (n_sp, cap, n_sp)
    ).reshape(slots, n_sp)
    place = lax.broadcasted_iota(jnp.int32, (slots, n_sp), 0) // cap
    receiver = wrap(place // n_x + y, n_y) * n_x + wrap(place % n_x + x, n_x)
    lane = lax.broadcasted_iota(jnp.int32, (slots, n_sp), 1)
    wanted = jnp.sum(jnp.where(lane == receiver, tiled, 0.0), axis=1, keepdims=True)
    local_rows = lat.shape[0]
    pick_wide = jnp.where(
        lax.broadcasted_iota(jnp.int32, (slots, local_rows), 1).astype(F32) == wanted, 1.0, 0.0
    )
    pick[...] = pick_wide.astype(BF16)
    loads[1].wait()
    blocks = to_blocks(dot(pick[...], lat[...]), n_sp).astype(BF16)
    out_rows[...] = blocks
    in_rows[0] = blocks[0]
    pl.semaphore_wait(barrier, n_sp + n_ens - 2)

    def space_exchange(src, dst, which):
        @pl.loop(0, n_sp - 1)
        def _(t):
            to, place, back_place = space_peer(t)
            remote(src.at[place], dst.at[back_place], which, {"space": to}).start()

    space_exchange(out_rows, in_rows, 0)

    loads[2].wait()
    loads[3].wait()
    grid_proj[...] = 0.5 * dot(emb[...], w_recv[...])
    pick_t[...] = jnp.transpose(pick_wide).astype(BF16)
    loads[4].wait()
    loads[5].wait()
    sender = slot_ref[...] // cap
    slot = (
        wrap(sender // n_x - y, n_y) * n_x + wrap(sender % n_x - x, n_x)
    ) * cap + slot_ref[...] % cap
    is_live = lax.broadcasted_iota(jnp.int32, slot.shape, 0) < count_ref[...]
    small[...] = jnp.zeros_like(small)
    small[0:per_point, :] = slot.astype(F32)
    small[per_point : 2 * per_point, :] = jnp.where(is_live, 1.0, 0.0)
    columns[...] = jnp.transpose(small[...])
    slot = jnp.where(is_live, slot, -1)
    slot_index = lax.broadcasted_iota(jnp.int32, (slots, part_points), 0)
    lane_index = lax.broadcasted_iota(jnp.int32, (points, slots), 1).astype(F32)
    for k in range(per_point):
        one_hot[k] = jnp.where(lane_index == columns[:, k : k + 1], 1.0, 0.0).astype(BF16)
        for h in range(PARTS):
            one_hot_t[h, :, k * part_points : (k + 1) * part_points] = jnp.where(
                slot_index == slot[k : k + 1, h * part_points : (h + 1) * part_points], 1.0, 0.0
            ).astype(BF16)
        live[k] = jnp.broadcast_to(
            columns[:, per_point + k : per_point + k + 1], (points, LANES)
        )
    loads[9].wait()
    variables = w_out_raw.shape[0]
    wide[...] = jnp.zeros_like(wide)
    wide[0:variables, :] = w_out_raw[...].astype(F32)
    w_out[...] = wide[...].astype(BF16)
    loads[10].wait()
    target_wide[...] = jnp.zeros_like(target_wide)
    target_wide[0:variables, :] = target_raw[...]
    target[...] = jnp.transpose(target_wide[...])
    loads[11].wait()
    var_wide[...] = jnp.zeros_like(var_wide)
    var_wide[0:1, 0:variables] = var_ref[...]
    loads[6].wait()
    loads[7].wait()
    loads[8].wait()

    step = 16

    def rows_of(h, i):
        return pl.ds(pl.multiple_of(h * part_points + i * step, step), step)

    def spread(k, rows):
        return jnp.concatenate([live[k, rows, :]] * (features // LANES), axis=1)

    def forward(h):
        span = pl.ds(h * part_points, part_points)
        for m in range(0, part_points, 128):
            rows = pl.ds(h * part_points + m, 128)
            for n in range(0, features, 256):
                lanes = pl.ds(n, 256)
                base = grid_proj[rows, lanes]
                total = jnp.zeros((128, 256), F32)
                for k in range(per_point):
                    u = dot(one_hot[k, rows, :], slot_proj[:, lanes]) + base
                    pre[k, rows, lanes] = u
                    mask = jnp.concatenate([live[k, rows, :]] * 2, axis=1)
                    total += silu(u) * mask
                summed_act[rows, lanes] = total.astype(BF16)

        node_in = (
            dot(summed_act[span, :], w_msg[...]) + emb[span, :].astype(F32)
        ).astype(BF16)
        u = 0.5 * dot(node_in, w_node[...])
        node_pre[span, :] = u
        hidden = silu(u).astype(BF16)
        pred[h] = dot_t(hidden, w_out[...]).reshape(pred.shape[1:]).astype(BF16)

        pred_in[h, 0] = pred[h, ens]

        @pl.loop(0, n_ens - 1)
        def _(t):
            q = from_far(t, n_ens)
            to = lax.rem(ens + q, n_ens)
            remote(pred.at[h, to], pred_in.at[h, n_ens - q], 1 + h, {"ens": to}).start()

    def slopes(h):
        @pl.loop(0, part_points // step)
        def _(i):
            rows = rows_of(h, i)
            base = grid_proj[rows, :]
            for k in range(per_point):
                pre[k, rows, :] = twice_slope(pre[k, rows, :])
            node_pre[rows, :] = 0.5 * twice_slope(node_pre[rows, :])

    def scores(h):
        whole(pred_in.at[h, pl.ds(1, n_ens - 1)], 1 + h).wait_recv()
        pred_wide[...] = pred_in[h].astype(F32)
        share = part_points // n_ens

        @pl.loop(0, share // 8)
        def _(i):
            rows = pl.ds(pl.multiple_of(i * 8, 8), 8)
            goal = target[
                pl.ds(pl.multiple_of(h * part_points + ens * share + i * 8, 8), 8), :
            ]
            mine = [pred_wide[m, rows, :] for m in range(n_ens)]
            pairwise = [jnp.zeros_like(goal) for _ in range(n_ens)]
            for a in range(n_ens):
                for b in range(a + 1, n_ens):
                    t = mine[a] - mine[b]
                    g = t * lax.rsqrt(t * t + SOFT)
                    pairwise[a] += g
                    pairwise[b] -= g
            weight_row = var_wide[0:1, :]
            for m in range(n_ens):
                t = mine[m] - goal
                g = t * lax.rsqrt(t * t + SOFT)
                grad_wide[m, rows, :] = weight_row * (g - pairwise[m] * (1.0 / (n_ens - 1.0)))

        grad_out[h] = grad_wide[...].astype(BF16)
        grad_in[h, 0] = grad_out[h, 0]

        @pl.loop(0, n_ens - 1)
        def _(t):
            q = from_far(t, n_ens)
            to = lax.rem(ens + q, n_ens)
            remote(
                grad_out.at[h, q], grad_in.at[h, n_ens - q], 1 + PARTS + h, {"ens": to}
            ).start()

    def edge_backward(h):
        whole(grad_in.at[h, pl.ds(1, n_ens - 1)], 1 + PARTS + h).wait_recv()

        @pl.loop(0, n_ens)
        def _(q):
            pred_grad[h, lax.rem(ens + q, n_ens)] = grad_in[h, q]

        span = pl.ds(h * part_points, part_points)
        hidden_grad = (
            dot(pred_grad[h].reshape(part_points, LANES), w_out[...]) * node_pre[span, :]
        ).astype(BF16)
        edge_grad[h] = dot_t(hidden_grad, w_node[...]).astype(BF16)

    def weight_half(which, h):
        return dot(summed_act_t[which, :, h * part_points : (h + 1) * part_points], edge_grad[h])

    def slot_backward(h):
        @pl.loop(0, part_points // step)
        def _(i):
            rows = rows_of(h, i)
            b = 0.5 * back[pl.ds(pl.multiple_of(i * step, step), step), :]
            for k in range(per_point):
                pre_grad[
                    pl.ds(pl.multiple_of(k * part_points + i * step, step), step), :
                ] = (b * pre[k, rows, :]).astype(BF16)

    whole(in_rows.at[pl.ds(1, n_sp - 1)], 0).wait_recv()
    arrived = from_blocks(in_rows[...].astype(F32)).astype(BF16)
    slot_proj[...] = (0.5 * dot(arrived, w_send[...])).astype(BF16)
    for h in range(PARTS):
        forward(h)

    for h in range(PARTS):
        slopes(h)
    turned = jnp.transpose(summed_act[...].astype(F32)).reshape(n_sp, 2, features // n_sp // 2, points)
    for c in range(2):
        summed_act_t[c] = turned[:, c].reshape(half, points).astype(BF16)

    for h in range(PARTS):
        scores(h)

    theirs, ours = 1 - core, core
    for h in range(PARTS - 1):
        edge_backward(h)
        back[...] = dot_t(edge_grad[h], w_msg[...])
        for i, which in enumerate((theirs, ours)):
            term = weight_half(which, h)
            halves[i] = term if h == 0 else halves[i] + term
        slot_backward(h)
        term = dot(one_hot_t[h], pre_grad[...])
        slot_grad[...] = term if h == 0 else slot_grad[...] + term

    last = PARTS - 1
    edge_backward(last)
    pair_out[...] = (halves[0] + weight_half(theirs, last)).astype(BF16)
    pair = remote(pair_out, pair_in, 7, {"ens": ens + 1 - 2 * core})
    pair.start()
    back[...] = dot_t(edge_grad[last], w_msg[...])
    own = halves[1] + weight_half(ours, last)
    halves[1] = own
    slot_backward(last)
    pair.wait_recv()
    blocks = to_blocks(halves[1] + pair_in[...].astype(F32), n_sp).astype(BF16)
    sum_out[...] = blocks
    sum_in[0] = sum_out[sp]

    @pl.loop(0, n_sp - 1)
    def _(t):
        to, _, back_place = space_peer(t)
        remote(sum_out.at[to], sum_in.at[back_place], 5, {"space": to}).start()

    blocks = to_blocks(
        slot_grad[...] + dot(one_hot_t[last], pre_grad[...]), n_sp
    ).astype(BF16)
    rows_out[...] = blocks
    rows_in[0] = blocks[0]
    space_exchange(rows_out, rows_in, 6)

    whole(sum_in.at[pl.ds(1, n_sp - 1)], 5).wait_recv()
    total_out[...] = jnp.sum(sum_in[...].astype(F32), axis=0).astype(BF16)
    total_in[0] = total_out[...]

    @pl.loop(0, n_ens - 1)
    def _(t):
        q = from_far(t, n_ens)
        to = lax.rem(ens + q, n_ens)
        remote(total_out, total_in.at[n_ens - q], 8, {"ens": to}).start()

    whole(rows_in.at[pl.ds(1, n_sp - 1)], 6).wait_recv()
    back_rows = from_blocks(rows_in[...].astype(F32)).astype(BF16)
    row_grads = dot(pick_t[...], back_rows)
    high = row_grads.astype(BF16)
    low = (row_grads - high.astype(F32)).astype(BF16)
    mesh_ref[...] = dot_t(high, w_send[...]) + dot_t(low, w_send[...])

    whole(total_in.at[pl.ds(1, n_ens - 1)], 8).wait_recv()
    same = total_in[0].astype(F32)
    other = total_in[1].astype(F32)
    for q in range(2, n_ens, 2):
        same += total_in[q].astype(F32)
        other += total_in[q + 1].astype(F32)
    first = jnp.where(core == 0, same, other)
    second = jnp.where(core == 0, other, same)
    weight_ref[...] = scale * jnp.concatenate(
        [from_blocks(first[None]), from_blocks(second[None])], axis=0
    )

    whole(out_rows.at[pl.ds(1, n_sp - 1)], 0).wait_send()
    for h in range(PARTS):
        whole(pred_in.at[h, pl.ds(1, n_ens - 1)], 1 + h).wait_send()
        whole(grad_out.at[h, pl.ds(1, n_ens - 1)], 1 + PARTS + h).wait_send()
    pair.wait_send()
    whole(sum_in.at[pl.ds(1, n_sp - 1)], 5).wait_send()
    whole(rows_out.at[pl.ds(1, n_sp - 1)], 6).wait_send()
    whole(total_in.at[pl.ds(1, n_ens - 1)], 8).wait_send()


def write_out(mesh_in, weight_in, mesh_ref, weight_ref, sem):
    copies = [
        pltpu.make_async_copy(mesh_in, mesh_ref, sem.at[0]),
        pltpu.make_async_copy(weight_in, weight_ref, sem.at[1]),
    ]
    for copy in copies:
        copy.start()
    for copy in copies:
        copy.wait()


def body(
    n_ens,
    n_sp,
    mesh_latent,
    grid_embed,
    w_send,
    w_recv,
    w_msg,
    w_node,
    w_out,
    target,
    var_weight,
    send_rows,
    edge_slot,
    edge_count,
):
    local_rows, features = mesh_latent.shape[1:]
    points, per_point = edge_slot.shape
    variables = target.shape[1]
    cap = send_rows.shape[2]
    slots = n_sp * cap
    part_points = points // PARTS
    share = part_points // n_ens
    half = features // 2
    out_block = features // n_sp
    total = n_ens * points * n_sp * per_point
    hbm = pl.BlockSpec(memory_space=pltpu.HBM)
    vmem = pl.BlockSpec(memory_space=pltpu.VMEM)
    square = (features, features)
    rows_blocks = (n_sp, 2 * cap, half)
    shares = (PARTS, n_ens, share, LANES)
    scratch = [
        pltpu.VMEM((local_rows, features), BF16),
        pltpu.VMEM((cap, n_sp), jnp.int32),
        pltpu.VMEM((points, features), BF16),
        pltpu.VMEM(square, BF16),
        pltpu.VMEM(square, BF16),
        pltpu.VMEM(square, BF16),
        pltpu.VMEM(square, BF16),
        pltpu.VMEM((variables, features), BF16),
        pltpu.VMEM((variables, points), F32),
        pltpu.VMEM((1, variables), F32),
        pltpu.VMEM((per_point, points), jnp.int32),
        pltpu.VMEM((1, points), jnp.int32),
        pltpu.VMEM((LANES, features), F32),
        pltpu.VMEM((LANES, features), BF16),
        pltpu.VMEM((LANES, points), F32),
        pltpu.VMEM((points, LANES), F32),
        pltpu.VMEM((8, LANES), F32),
        pltpu.VMEM((LANES, points), F32),
        pltpu.VMEM((points, LANES), F32),
        pltpu.VMEM((slots, local_rows), BF16),
        pltpu.VMEM((local_rows, slots), BF16),
        pltpu.VMEM(rows_blocks, BF16),
        pltpu.VMEM(rows_blocks, BF16),
        pltpu.VMEM((slots, features), BF16),
        pltpu.VMEM((points, features), F32),
        pltpu.VMEM((per_point, points, slots), BF16),
        pltpu.VMEM((PARTS, slots, per_point * part_points), BF16),
        pltpu.VMEM((per_point, points, features), F32),
        pltpu.VMEM((per_point, points, LANES), F32),
        pltpu.VMEM((points, features), BF16),
        pltpu.VMEM((2, half, points), BF16),
        pltpu.VMEM((points, features), F32),
        pltpu.VMEM(shares, BF16),
        pltpu.VMEM(shares, BF16),
        pltpu.VMEM(shares[1:], F32),
        pltpu.VMEM(shares[1:], F32),
        pltpu.VMEM(shares, BF16),
        pltpu.VMEM(shares, BF16),
        pltpu.VMEM(shares, BF16),
        pltpu.VMEM((PARTS, part_points, features), BF16),
        pltpu.VMEM((part_points, features), F32),
        pltpu.VMEM((per_point * part_points, features), BF16),
        pltpu.VMEM((slots, features), F32),
        pltpu.VMEM((2, half, features), F32),
        pltpu.VMEM((half, features), BF16),
        pltpu.VMEM((half, features), BF16),
        pltpu.VMEM((n_sp, out_block, half), BF16),
        pltpu.VMEM((n_sp, out_block, half), BF16),
        pltpu.VMEM((out_block, half), BF16),
        pltpu.VMEM((n_ens, out_block, half), BF16),
        pltpu.VMEM(rows_blocks, BF16),
        pltpu.VMEM(rows_blocks, BF16),
        pltpu.SemaphoreType.DMA((12,)),
        pltpu.SemaphoreType.DMA((9,)),
        pltpu.SemaphoreType.DMA((9,)),
    ]
    mesh_grad, weight_grad = pl.pallas_call(
        functools.partial(kernel, n_ens, n_sp, 1.0 / math.sqrt(total)),
        out_shape=(
            pltpu.VMEM((local_rows, features), F32),
            pltpu.VMEM((out_block, features), F32),
        ),
        in_specs=[hbm] * 12,
        out_specs=(vmem, vmem),
        scratch_shapes=scratch,
        compiler_params=pltpu.CompilerParams(
            collective_id=0, has_side_effects=True, vmem_limit_bytes=48 * 1024 * 1024
        ),
    )(
        *(
            pltpu.with_memory_space_constraint(array, pltpu.HBM)
            for array in (
                mesh_latent[0],
                grid_embed,
                w_send,
                w_recv,
                w_msg,
                w_node,
                w_out.T,
                target.T,
                var_weight.reshape(1, variables),
                jnp.swapaxes(send_rows[0], 0, 1),
                edge_slot.T,
                edge_count.reshape(1, points),
            )
        )
    )
    mesh_grad, weight_grad = pl.pallas_call(
        write_out,
        out_shape=(
            jax.ShapeDtypeStruct((local_rows, features), F32),
            jax.ShapeDtypeStruct((out_block, features), F32),
        ),
        in_specs=[vmem] * 2,
        out_specs=(hbm, hbm),
        scratch_shapes=[pltpu.SemaphoreType.DMA((2,))],
    )(
        pltpu.with_memory_space_constraint(mesh_grad, pltpu.VMEM),
        pltpu.with_memory_space_constraint(weight_grad, pltpu.VMEM),
    )
    return (mesh_grad[None], weight_grad)


def solution(mesh):
    in_specs = (
        P("ens", "space", None),
        P("space", None),
        P(),
        P(),
        P(),
        P(),
        P(),
        P("space", None),
        P(),
        P("space", None, None),
        P("space", None),
        P("space"),
    )
    out_specs = (P("ens", "space", None), P("space", None))
    return jax.shard_map(
        functools.partial(body, mesh.shape["ens"], mesh.shape["space"]),
        mesh=mesh,
        in_specs=in_specs,
        out_specs=out_specs,
        check_vma=False,
    )
```

```python
import functools
import math

import jax
import jax.numpy as jnp
from jax import lax
from jax.experimental import pallas as pl
from jax.experimental.pallas import tpu as pltpu
from jax.sharding import PartitionSpec as P

MESH = pl.DeviceIdType.MESH
F32 = jnp.float32
BF16 = jnp.bfloat16
SOFT = 0.09
LANES = 128
ALONG_X = 4
PARTS = 2


def silu(u):
    return u * jnp.tanh(u) + u


def twice_slope(u):
    t = jnp.tanh(u)
    return 1.0 + t + u * (1.0 - t * t)


def dot(a, b):
    return jnp.dot(a, b, preferred_element_type=F32)


def dot_t(a, b):
    return lax.dot_general(a, b, (((1,), (1,)), ((), ())), preferred_element_type=F32)


def to_blocks(rows, n):
    c, f = rows.shape[0] // n, rows.shape[1]
    split = rows.reshape(n, c, f)
    return jnp.concatenate([split[:, :, : f // 2], split[:, :, f // 2 :]], axis=1)


def from_blocks(blocks):
    n, c2, f2 = blocks.shape
    c = c2 // 2
    left = blocks[:, :c, :].reshape(n * c, f2)
    right = blocks[:, c:, :].reshape(n * c, f2)
    return jnp.concatenate([left, right], axis=1)


def wrap(i, n):
    return jnp.where(i < 0, i + n, jnp.where(i >= n, i - n, i))


def kernel(
    n_ens,
    n_sp,
    scale,
    lat_h,
    emb_h,
    w_send_h,
    w_recv_h,
    w_msg_h,
    w_node_h,
    w_out_h,
    target_h,
    var_h,
    rows_h,
    slot_h,
    count_h,
    mesh_ref,
    weight_ref,
    lat,
    rows_ref,
    emb,
    w_send,
    w_recv,
    w_msg,
    w_node,
    w_out_raw,
    target_raw,
    var_ref,
    slot_ref,
    count_ref,
    wide,
    w_out,
    target_wide,
    target,
    var_wide,
    small,
    columns,
    pick,
    pick_t,
    out_rows,
    in_rows,
    slot_proj,
    grid_proj,
    one_hot,
    one_hot_t,
    pre,
    live,
    summed_act,
    summed_act_t,
    node_pre,
    pred,
    pred_in,
    pred_wide,
    grad_wide,
    grad_out,
    grad_in,
    pred_grad,
    edge_grad,
    back,
    pre_grad,
    slot_grad,
    halves,
    pair_out,
    pair_in,
    sum_out,
    sum_in,
    total_out,
    total_in,
    rows_out,
    rows_in,
    load_sem,
    send_sem,
    recv_sem,
):
    ens = lax.axis_index("ens")
    sp = lax.axis_index("space")
    core = lax.rem(ens, 2)
    n_x = ALONG_X
    n_y = n_sp // n_x
    y = lax.div(sp, n_x)
    x = lax.rem(sp, n_x)
    points, features = emb.shape
    per_point = slot_ref.shape[0]
    cap = rows_ref.shape[0]
    slots = n_sp * cap
    part_points = points // PARTS
    half = features // 2

    def hops(d, n):
        return min(d, n - d)

    rows_of_y = [lax.rem(y + dy, n_y) * n_x for dy in range(n_y)]
    columns_of_x = [lax.rem(x + dx, n_x) for dx in range(n_x)]
    offsets = [(dy, dx) for dy in range(n_y) for dx in range(n_x) if (dy, dx) != (0, 0)]
    offsets.sort(key=lambda d: -hops(d[0], n_y) - hops(d[1], n_x))
    space_peers = [
        (rows_of_y[dy] + columns_of_x[dx], dy * n_x + dx, (n_y - dy) % n_y * n_x + (n_x - dx) % n_x)
        for dy, dx in offsets
    ]
    ens_offsets = sorted(range(1, n_ens), key=lambda q: -hops(q // 2, n_ens // 2))
    ens_peers = [(lax.rem(ens + q, n_ens), q) for q in ens_offsets]

    barrier = pltpu.get_barrier_semaphore()

    for to, _, _ in space_peers:
        pl.semaphore_signal(barrier, inc=1, device_id={"space": to}, device_id_type=MESH)

    for to, _ in ens_peers:
        pl.semaphore_signal(barrier, inc=1, device_id={"ens": to}, device_id_type=MESH)

    loads = [
        pltpu.make_async_copy(src, dst, load_sem.at[i])
        for i, (src, dst) in enumerate(
            [
                (rows_h, rows_ref),
                (lat_h, lat),
                (emb_h, emb),
                (w_recv_h, w_recv),
                (slot_h, slot_ref),
                (count_h, count_ref),
                (w_send_h, w_send),
                (w_msg_h, w_msg),
                (w_node_h, w_node),
                (w_out_h, w_out_raw),
                (target_h, target_raw),
                (var_h, var_ref),
            ]
        )
    ]
    for load in loads:
        load.start()

    def remote(src, dst, which, to):
        return pltpu.make_async_remote_copy(
            src_ref=src,
            dst_ref=dst,
            send_sem=send_sem.at[which],
            recv_sem=recv_sem.at[which],
            device_id=to,
            device_id_type=MESH,
        )

    def whole(ref, which):
        return remote(ref, ref, which, {"ens": ens})

    loads[0].wait()
    tiled = jnp.broadcast_to(
        rows_ref[...].astype(F32)[None], (n_sp, cap, n_sp)
    ).reshape(slots, n_sp)
    place = lax.broadcasted_iota(jnp.int32, (slots, n_sp), 0) // cap
    receiver = wrap(place // n_x + y, n_y) * n_x + wrap(place % n_x + x, n_x)
    lane = lax.broadcasted_iota(jnp.int32, (slots, n_sp), 1)
    wanted = jnp.sum(jnp.where(lane == receiver, tiled, 0.0), axis=1, keepdims=True)
    local_rows = lat.shape[0]
    pick_wide = jnp.where(
        lax.broadcasted_iota(jnp.int32, (slots, local_rows), 1).astype(F32) == wanted, 1.0, 0.0
    )
    pick[...] = pick_wide.astype(BF16)
    loads[1].wait()
    blocks = to_blocks(dot(pick[...], lat[...]), n_sp).astype(BF16)
    out_rows[...] = blocks
    in_rows[0] = blocks[0]
    pl.semaphore_wait(barrier, n_sp + n_ens - 2)

    def space_exchange(src, dst, which):
        for to, place, back_place in space_peers:
            remote(src.at[place], dst.at[back_place], which, {"space": to}).start()

    space_exchange(out_rows, in_rows, 0)

    loads[2].wait()
    loads[3].wait()
    grid_proj[...] = 0.5 * dot(emb[...], w_recv[...])
    pick_t[...] = jnp.transpose(pick_wide).astype(BF16)
    loads[4].wait()
    loads[5].wait()
    sender = slot_ref[...] // cap
    slot = (
        wrap(sender // n_x - y, n_y) * n_x + wrap(sender % n_x - x, n_x)
    ) * cap + slot_ref[...] % cap
    is_live = lax.broadcasted_iota(jnp.int32, slot.shape, 0) < count_ref[...]
    small[...] = jnp.zeros_like(small)
    small[0:per_point, :] = slot.astype(F32)
    small[per_point : 2 * per_point, :] = jnp.where(is_live, 1.0, 0.0)
    columns[...] = jnp.transpose(small[...])
    slot = jnp.where(is_live, slot, -1)
    slot_index = lax.broadcasted_iota(jnp.int32, (slots, part_points), 0)
    lane_index = lax.broadcasted_iota(jnp.int32, (points, slots), 1).astype(F32)
    for k in range(per_point):
        one_hot[k] = jnp.where(lane_index == columns[:, k : k + 1], 1.0, 0.0).astype(BF16)
        for h in range(PARTS):
            one_hot_t[h, :, k * part_points : (k + 1) * part_points] = jnp.where(
                slot_index == slot[k : k + 1, h * part_points : (h + 1) * part_points], 1.0, 0.0
            ).astype(BF16)
        live[k] = jnp.broadcast_to(
            columns[:, per_point + k : per_point + k + 1], (points, LANES)
        )
    loads[9].wait()
    variables = w_out_raw.shape[0]
    wide[...] = jnp.zeros_like(wide)
    wide[0:variables, :] = w_out_raw[...].astype(F32)
    w_out[...] = wide[...].astype(BF16)
    loads[10].wait()
    target_wide[...] = jnp.zeros_like(target_wide)
    target_wide[0:variables, :] = target_raw[...]
    target[...] = jnp.transpose(target_wide[...])
    loads[11].wait()
    var_wide[...] = jnp.zeros_like(var_wide)
    var_wide[0:1, 0:variables] = var_ref[...]
    loads[6].wait()
    loads[7].wait()
    loads[8].wait()

    step = 16

    def rows_of(h, i):
        return pl.ds(pl.multiple_of(h * part_points + i * step, step), step)

    def spread(k, rows):
        return jnp.concatenate([live[k, rows, :]] * (features // LANES), axis=1)

    def forward(h):
        span = pl.ds(h * part_points, part_points)
        for m in range(0, part_points, 128):
            rows = pl.ds(h * part_points + m, 128)
            for n in range(0, features, 256):
                lanes = pl.ds(n, 256)
                base = grid_proj[rows, lanes]
                total = jnp.zeros((128, 256), F32)
                for k in range(per_point):
                    u = dot(one_hot[k, rows, :], slot_proj[:, lanes]) + base
                    pre[k, rows, lanes] = u
                    mask = jnp.concatenate([live[k, rows, :]] * 2, axis=1)
                    total += silu(u) * mask
                summed_act[rows, lanes] = total.astype(BF16)

        node_in = (
            dot(summed_act[span, :], w_msg[...]) + emb[span, :].astype(F32)
        ).astype(BF16)
        u = 0.5 * dot(node_in, w_node[...])
        node_pre[span, :] = u
        hidden = silu(u).astype(BF16)
        pred[h] = dot_t(hidden, w_out[...]).reshape(pred.shape[1:]).astype(BF16)

        pred_in[h, 0] = pred[h, ens]

        for to, q in ens_peers:
            remote(pred.at[h, to], pred_in.at[h, n_ens - q], 1 + h, {"ens": to}).start()

    def slopes(h):
        @pl.loop(0, part_points // step)
        def _(i):
            rows = rows_of(h, i)
            base = grid_proj[rows, :]
            for k in range(per_point):
                pre[k, rows, :] = twice_slope(pre[k, rows, :])
            node_pre[rows, :] = 0.5 * twice_slope(node_pre[rows, :])

    def scores(h):
        whole(pred_in.at[h, pl.ds(1, n_ens - 1)], 1 + h).wait_recv()
        pred_wide[...] = pred_in[h].astype(F32)
        share = part_points // n_ens

        @pl.loop(0, share // 8)
        def _(i):
            rows = pl.ds(pl.multiple_of(i * 8, 8), 8)
            goal = target[
                pl.ds(pl.multiple_of(h * part_points + ens * share + i * 8, 8), 8), :
            ]
            mine = [pred_wide[m, rows, :] for m in range(n_ens)]
            pairwise = [jnp.zeros_like(goal) for _ in range(n_ens)]
            for a in range(n_ens):
                for b in range(a + 1, n_ens):
                    t = mine[a] - mine[b]
                    g = t * lax.rsqrt(t * t + SOFT)
                    pairwise[a] += g
                    pairwise[b] -= g
            weight_row = var_wide[0:1, :]
            for m in range(n_ens):
                t = mine[m] - goal
                g = t * lax.rsqrt(t * t + SOFT)
                grad_wide[m, rows, :] = weight_row * (g - pairwise[m] * (1.0 / (n_ens - 1.0)))

        grad_out[h] = grad_wide[...].astype(BF16)
        grad_in[h, 0] = grad_out[h, 0]

        for to, q in ens_peers:
            remote(
                grad_out.at[h, q], grad_in.at[h, n_ens - q], 1 + PARTS + h, {"ens": to}
            ).start()

    def edge_backward(h):
        whole(grad_in.at[h, pl.ds(1, n_ens - 1)], 1 + PARTS + h).wait_recv()

        @pl.loop(0, n_ens)
        def _(q):
            pred_grad[h, lax.rem(ens + q, n_ens)] = grad_in[h, q]

        span = pl.ds(h * part_points, part_points)
        hidden_grad = (
            dot(pred_grad[h].reshape(part_points, LANES), w_out[...]) * node_pre[span, :]
        ).astype(BF16)
        edge_grad[h] = dot_t(hidden_grad, w_node[...]).astype(BF16)

    def weight_half(which, h):
        return dot(summed_act_t[which, :, h * part_points : (h + 1) * part_points], edge_grad[h])

    def slot_backward(h):
        @pl.loop(0, part_points // step)
        def _(i):
            rows = rows_of(h, i)
            b = 0.5 * back[pl.ds(pl.multiple_of(i * step, step), step), :]
            for k in range(per_point):
                pre_grad[
                    pl.ds(pl.multiple_of(k * part_points + i * step, step), step), :
                ] = (b * pre[k, rows, :]).astype(BF16)

    whole(in_rows.at[pl.ds(1, n_sp - 1)], 0).wait_recv()
    arrived = from_blocks(in_rows[...].astype(F32)).astype(BF16)
    slot_proj[...] = (0.5 * dot(arrived, w_send[...])).astype(BF16)
    for h in range(PARTS):
        forward(h)

    for h in range(PARTS):
        slopes(h)
    turned = jnp.transpose(summed_act[...].astype(F32)).reshape(n_sp, 2, features // n_sp // 2, points)
    for c in range(2):
        summed_act_t[c] = turned[:, c].reshape(half, points).astype(BF16)

    for h in range(PARTS):
        scores(h)

    theirs, ours = 1 - core, core
    for h in range(PARTS - 1):
        edge_backward(h)
        back[...] = dot_t(edge_grad[h], w_msg[...])
        for i, which in enumerate((theirs, ours)):
            term = weight_half(which, h)
            halves[i] = term if h == 0 else halves[i] + term
        slot_backward(h)
        term = dot(one_hot_t[h], pre_grad[...])
        slot_grad[...] = term if h == 0 else slot_grad[...] + term

    last = PARTS - 1
    edge_backward(last)
    pair_out[...] = (halves[0] + weight_half(theirs, last)).astype(BF16)
    pair = remote(pair_out, pair_in, 7, {"ens": ens + 1 - 2 * core})
    pair.start()
    back[...] = dot_t(edge_grad[last], w_msg[...])
    own = halves[1] + weight_half(ours, last)
    halves[1] = own
    slot_backward(last)
    pair.wait_recv()
    blocks = to_blocks(halves[1] + pair_in[...].astype(F32), n_sp).astype(BF16)
    sum_out[...] = blocks
    sum_in[0] = sum_out[sp]

    for to, _, back_place in space_peers:
        remote(sum_out.at[to], sum_in.at[back_place], 5, {"space": to}).start()

    blocks = to_blocks(
        slot_grad[...] + dot(one_hot_t[last], pre_grad[...]), n_sp
    ).astype(BF16)
    rows_out[...] = blocks
    rows_in[0] = blocks[0]
    space_exchange(rows_out, rows_in, 6)

    whole(sum_in.at[pl.ds(1, n_sp - 1)], 5).wait_recv()
    total_out[...] = jnp.sum(sum_in[...].astype(F32), axis=0).astype(BF16)
    total_in[0] = total_out[...]

    for to, q in ens_peers:
        remote(total_out, total_in.at[n_ens - q], 8, {"ens": to}).start()

    whole(rows_in.at[pl.ds(1, n_sp - 1)], 6).wait_recv()
    back_rows = from_blocks(rows_in[...].astype(F32)).astype(BF16)
    row_grads = dot(pick_t[...], back_rows)
    high = row_grads.astype(BF16)
    low = (row_grads - high.astype(F32)).astype(BF16)
    mesh_ref[...] = dot_t(high, w_send[...]) + dot_t(low, w_send[...])

    whole(total_in.at[pl.ds(1, n_ens - 1)], 8).wait_recv()
    same = total_in[0].astype(F32)
    other = total_in[1].astype(F32)
    for q in range(2, n_ens, 2):
        same += total_in[q].astype(F32)
        other += total_in[q + 1].astype(F32)
    first = jnp.where(core == 0, same, other)
    second = jnp.where(core == 0, other, same)
    weight_ref[...] = scale * jnp.concatenate(
        [from_blocks(first[None]), from_blocks(second[None])], axis=0
    )

    whole(out_rows.at[pl.ds(1, n_sp - 1)], 0).wait_send()
    for h in range(PARTS):
        whole(pred_in.at[h, pl.ds(1, n_ens - 1)], 1 + h).wait_send()
        whole(grad_out.at[h, pl.ds(1, n_ens - 1)], 1 + PARTS + h).wait_send()
    pair.wait_send()
    whole(sum_in.at[pl.ds(1, n_sp - 1)], 5).wait_send()
    whole(rows_out.at[pl.ds(1, n_sp - 1)], 6).wait_send()
    whole(total_in.at[pl.ds(1, n_ens - 1)], 8).wait_send()


def write_out(mesh_in, weight_in, mesh_ref, weight_ref, sem):
    copies = [
        pltpu.make_async_copy(mesh_in, mesh_ref, sem.at[0]),
        pltpu.make_async_copy(weight_in, weight_ref, sem.at[1]),
    ]
    for copy in copies:
        copy.start()
    for copy in copies:
        copy.wait()


def body(
    n_ens,
    n_sp,
    mesh_latent,
    grid_embed,
    w_send,
    w_recv,
    w_msg,
    w_node,
    w_out,
    target,
    var_weight,
    send_rows,
    edge_slot,
    edge_count,
):
    local_rows, features = mesh_latent.shape[1:]
    points, per_point = edge_slot.shape
    variables = target.shape[1]
    cap = send_rows.shape[2]
    slots = n_sp * cap
    part_points = points // PARTS
    share = part_points // n_ens
    half = features // 2
    out_block = features // n_sp
    total = n_ens * points * n_sp * per_point
    hbm = pl.BlockSpec(memory_space=pltpu.HBM)
    vmem = pl.BlockSpec(memory_space=pltpu.VMEM)
    square = (features, features)
    rows_blocks = (n_sp, 2 * cap, half)
    shares = (PARTS, n_ens, share, LANES)
    scratch = [
        pltpu.VMEM((local_rows, features), BF16),
        pltpu.VMEM((cap, n_sp), jnp.int32),
        pltpu.VMEM((points, features), BF16),
        pltpu.VMEM(square, BF16),
        pltpu.VMEM(square, BF16),
        pltpu.VMEM(square, BF16),
        pltpu.VMEM(square, BF16),
        pltpu.VMEM((variables, features), BF16),
        pltpu.VMEM((variables, points), F32),
        pltpu.VMEM((1, variables), F32),
        pltpu.VMEM((per_point, points), jnp.int32),
        pltpu.VMEM((1, points), jnp.int32),
        pltpu.VMEM((LANES, features), F32),
        pltpu.VMEM((LANES, features), BF16),
        pltpu.VMEM((LANES, points), F32),
        pltpu.VMEM((points, LANES), F32),
        pltpu.VMEM((8, LANES), F32),
        pltpu.VMEM((LANES, points), F32),
        pltpu.VMEM((points, LANES), F32),
        pltpu.VMEM((slots, local_rows), BF16),
        pltpu.VMEM((local_rows, slots), BF16),
        pltpu.VMEM(rows_blocks, BF16),
        pltpu.VMEM(rows_blocks, BF16),
        pltpu.VMEM((slots, features), BF16),
        pltpu.VMEM((points, features), F32),
        pltpu.VMEM((per_point, points, slots), BF16),
        pltpu.VMEM((PARTS, slots, per_point * part_points), BF16),
        pltpu.VMEM((per_point, points, features), F32),
        pltpu.VMEM((per_point, points, LANES), F32),
        pltpu.VMEM((points, features), BF16),
        pltpu.VMEM((2, half, points), BF16),
        pltpu.VMEM((points, features), F32),
        pltpu.VMEM(shares, BF16),
        pltpu.VMEM(shares, BF16),
        pltpu.VMEM(shares[1:], F32),
        pltpu.VMEM(shares[1:], F32),
        pltpu.VMEM(shares, BF16),
        pltpu.VMEM(shares, BF16),
        pltpu.VMEM(shares, BF16),
        pltpu.VMEM((PARTS, part_points, features), BF16),
        pltpu.VMEM((part_points, features), F32),
        pltpu.VMEM((per_point * part_points, features), BF16),
        pltpu.VMEM((slots, features), F32),
        pltpu.VMEM((2, half, features), F32),
        pltpu.VMEM((half, features), BF16),
        pltpu.VMEM((half, features), BF16),
        pltpu.VMEM((n_sp, out_block, half), BF16),
        pltpu.VMEM((n_sp, out_block, half), BF16),
        pltpu.VMEM((out_block, half), BF16),
        pltpu.VMEM((n_ens, out_block, half), BF16),
        pltpu.VMEM(rows_blocks, BF16),
        pltpu.VMEM(rows_blocks, BF16),
        pltpu.SemaphoreType.DMA((12,)),
        pltpu.SemaphoreType.DMA((9,)),
        pltpu.SemaphoreType.DMA((9,)),
    ]
    mesh_grad, weight_grad = pl.pallas_call(
        functools.partial(kernel, n_ens, n_sp, 1.0 / math.sqrt(total)),
        out_shape=(
            pltpu.VMEM((local_rows, features), F32),
            pltpu.VMEM((out_block, features), F32),
        ),
        in_specs=[hbm] * 12,
        out_specs=(vmem, vmem),
        scratch_shapes=scratch,
        compiler_params=pltpu.CompilerParams(
            collective_id=0, has_side_effects=True, vmem_limit_bytes=48 * 1024 * 1024
        ),
    )(
        *(
            pltpu.with_memory_space_constraint(array, pltpu.HBM)
            for array in (
                mesh_latent[0],
                grid_embed,
                w_send,
                w_recv,
                w_msg,
                w_node,
                w_out.T,
                target.T,
                var_weight.reshape(1, variables),
                jnp.swapaxes(send_rows[0], 0, 1),
                edge_slot.T,
                edge_count.reshape(1, points),
            )
        )
    )
    mesh_grad, weight_grad = pl.pallas_call(
        write_out,
        out_shape=(
            jax.ShapeDtypeStruct((local_rows, features), F32),
            jax.ShapeDtypeStruct((out_block, features), F32),
        ),
        in_specs=[vmem] * 2,
        out_specs=(hbm, hbm),
        scratch_shapes=[pltpu.SemaphoreType.DMA((2,))],
    )(
        pltpu.with_memory_space_constraint(mesh_grad, pltpu.VMEM),
        pltpu.with_memory_space_constraint(weight_grad, pltpu.VMEM),
    )
    return (mesh_grad[None], weight_grad)


def solution(mesh):
    in_specs = (
        P("ens", "space", None),
        P("space", None),
        P(),
        P(),
        P(),
        P(),
        P(),
        P("space", None),
        P(),
        P("space", None, None),
        P("space", None),
        P("space"),
    )
    out_specs = (P("ens", "space", None), P("space", None))
    return jax.shard_map(
        functools.partial(body, mesh.shape["ens"], mesh.shape["space"]),
        mesh=mesh,
        in_specs=in_specs,
        out_specs=out_specs,
        check_vma=False,
    )
```

```python
import functools
import math

import jax
import jax.numpy as jnp
from jax import lax
from jax.experimental import pallas as pl
from jax.experimental.pallas import tpu as pltpu
from jax.sharding import PartitionSpec as P

MESH = pl.DeviceIdType.MESH
F32 = jnp.float32
BF16 = jnp.bfloat16
SOFT = 0.09
LANES = 128
ALONG_X = 4
PARTS = 2


def sigmoid(v):
    return 1.0 / (1.0 + jnp.exp(-v))


def silu(v):
    return v * sigmoid(v)


def slope(v):
    s = sigmoid(v)
    return s * (1.0 + v * (1.0 - s))


def dot(a, b):
    return jnp.dot(a, b, preferred_element_type=F32)


def dot_t(a, b):
    return lax.dot_general(a, b, (((1,), (1,)), ((), ())), preferred_element_type=F32)


def to_blocks(rows, n):
    c, f = rows.shape[0] // n, rows.shape[1]
    split = rows.reshape(n, c, f)
    return jnp.concatenate([split[:, :, : f // 2], split[:, :, f // 2 :]], axis=1)


def from_blocks(blocks):
    n, c2, f2 = blocks.shape
    c = c2 // 2
    left = blocks[:, :c, :].reshape(n * c, f2)
    right = blocks[:, c:, :].reshape(n * c, f2)
    return jnp.concatenate([left, right], axis=1)


def wrap(i, n):
    return jnp.where(i < 0, i + n, jnp.where(i >= n, i - n, i))


def kernel(
    n_ens,
    n_sp,
    scale,
    lat_h,
    emb_h,
    w_send_h,
    w_recv_h,
    w_msg_h,
    w_node_h,
    w_out_h,
    target_h,
    var_h,
    rows_h,
    slot_h,
    count_h,
    mesh_ref,
    weight_ref,
    lat,
    rows_ref,
    emb,
    w_send,
    w_recv,
    w_msg,
    w_node,
    w_out_raw,
    target_raw,
    var_ref,
    slot_ref,
    count_ref,
    wide,
    w_out,
    target_wide,
    target,
    var_wide,
    small,
    columns,
    pick,
    pick_t,
    out_rows,
    in_rows,
    slot_proj,
    grid_proj,
    one_hot,
    one_hot_t,
    pre,
    live,
    summed_act,
    summed_act_t,
    node_pre,
    pred,
    pred_in,
    pred_wide,
    grad_wide,
    grad_out,
    grad_in,
    pred_grad,
    edge_grad,
    back,
    pre_grad,
    slot_grad,
    halves,
    pair_out,
    pair_in,
    sum_out,
    sum_in,
    total_out,
    total_in,
    rows_out,
    rows_in,
    load_sem,
    send_sem,
    recv_sem,
):
    ens = lax.axis_index("ens")
    sp = lax.axis_index("space")
    core = lax.rem(ens, 2)
    n_x = ALONG_X
    n_y = n_sp // n_x
    y = lax.div(sp, n_x)
    x = lax.rem(sp, n_x)
    points, features = emb.shape
    per_point = slot_ref.shape[0]
    cap = rows_ref.shape[0]
    slots = n_sp * cap
    part_points = points // PARTS
    half = features // 2

    def hops(d, n):
        return min(d, n - d)

    rows_of_y = [lax.rem(y + dy, n_y) * n_x for dy in range(n_y)]
    columns_of_x = [lax.rem(x + dx, n_x) for dx in range(n_x)]
    offsets = [(dy, dx) for dy in range(n_y) for dx in range(n_x) if (dy, dx) != (0, 0)]
    offsets.sort(key=lambda d: -hops(d[0], n_y) - hops(d[1], n_x))
    space_peers = [
        (rows_of_y[dy] + columns_of_x[dx], dy * n_x + dx, (n_y - dy) % n_y * n_x + (n_x - dx) % n_x)
        for dy, dx in offsets
    ]
    ens_offsets = sorted(range(1, n_ens), key=lambda q: -hops(q // 2, n_ens // 2))
    ens_peers = [(lax.rem(ens + q, n_ens), q) for q in ens_offsets]

    barrier = pltpu.get_barrier_semaphore()

    for to, _, _ in space_peers:
        pl.semaphore_signal(barrier, inc=1, device_id={"space": to}, device_id_type=MESH)

    for to, _ in ens_peers:
        pl.semaphore_signal(barrier, inc=1, device_id={"ens": to}, device_id_type=MESH)

    loads = [
        pltpu.make_async_copy(src, dst, load_sem.at[i])
        for i, (src, dst) in enumerate(
            [
                (rows_h, rows_ref),
                (lat_h, lat),
                (emb_h, emb),
                (w_recv_h, w_recv),
                (slot_h, slot_ref),
                (count_h, count_ref),
                (w_send_h, w_send),
                (w_msg_h, w_msg),
                (w_node_h, w_node),
                (w_out_h, w_out_raw),
                (target_h, target_raw),
                (var_h, var_ref),
            ]
        )
    ]
    for load in loads:
        load.start()

    def remote(src, dst, which, to):
        return pltpu.make_async_remote_copy(
            src_ref=src,
            dst_ref=dst,
            send_sem=send_sem.at[which],
            recv_sem=recv_sem.at[which],
            device_id=to,
            device_id_type=MESH,
        )

    def whole(ref, which):
        return remote(ref, ref, which, {"ens": ens})

    loads[0].wait()
    tiled = jnp.broadcast_to(
        rows_ref[...].astype(F32)[None], (n_sp, cap, n_sp)
    ).reshape(slots, n_sp)
    place = lax.broadcasted_iota(jnp.int32, (slots, n_sp), 0) // cap
    receiver = wrap(place // n_x + y, n_y) * n_x + wrap(place % n_x + x, n_x)
    lane = lax.broadcasted_iota(jnp.int32, (slots, n_sp), 1)
    wanted = jnp.sum(jnp.where(lane == receiver, tiled, 0.0), axis=1, keepdims=True)
    local_rows = lat.shape[0]
    pick_wide = jnp.where(
        lax.broadcasted_iota(jnp.int32, (slots, local_rows), 1).astype(F32) == wanted, 1.0, 0.0
    )
    pick[...] = pick_wide.astype(BF16)
    loads[1].wait()
    blocks = to_blocks(dot(pick[...], lat[...]), n_sp).astype(BF16)
    out_rows[...] = blocks
    in_rows[0] = blocks[0]
    pl.semaphore_wait(barrier, n_sp + n_ens - 2)

    def space_exchange(src, dst, which):
        for to, place, back_place in space_peers:
            remote(src.at[place], dst.at[back_place], which, {"space": to}).start()

    space_exchange(out_rows, in_rows, 0)

    loads[2].wait()
    loads[3].wait()
    grid_proj[...] = dot(emb[...], w_recv[...])
    pick_t[...] = jnp.transpose(pick_wide).astype(BF16)
    loads[4].wait()
    loads[5].wait()
    sender = slot_ref[...] // cap
    slot = (
        wrap(sender // n_x - y, n_y) * n_x + wrap(sender % n_x - x, n_x)
    ) * cap + slot_ref[...] % cap
    is_live = lax.broadcasted_iota(jnp.int32, slot.shape, 0) < count_ref[...]
    small[...] = jnp.zeros_like(small)
    small[0:per_point, :] = slot.astype(F32)
    small[per_point : 2 * per_point, :] = jnp.where(is_live, 1.0, 0.0)
    columns[...] = jnp.transpose(small[...])
    slot = jnp.where(is_live, slot, -1)
    slot_index = lax.broadcasted_iota(jnp.int32, (slots, part_points), 0)
    lane_index = lax.broadcasted_iota(jnp.int32, (points, slots), 1).astype(F32)
    for k in range(per_point):
        one_hot[k] = jnp.where(lane_index == columns[:, k : k + 1], 1.0, 0.0).astype(BF16)
        for h in range(PARTS):
            one_hot_t[h, :, k * part_points : (k + 1) * part_points] = jnp.where(
                slot_index == slot[k : k + 1, h * part_points : (h + 1) * part_points], 1.0, 0.0
            ).astype(BF16)
        live[k] = jnp.broadcast_to(
            columns[:, per_point + k : per_point + k + 1], (points, LANES)
        )
    loads[9].wait()
    variables = w_out_raw.shape[0]
    wide[...] = jnp.zeros_like(wide)
    wide[0:variables, :] = w_out_raw[...].astype(F32)
    w_out[...] = wide[...].astype(BF16)
    loads[10].wait()
    target_wide[...] = jnp.zeros_like(target_wide)
    target_wide[0:variables, :] = target_raw[...]
    target[...] = jnp.transpose(target_wide[...])
    loads[11].wait()
    var_wide[...] = jnp.zeros_like(var_wide)
    var_wide[0:1, 0:variables] = var_ref[...]
    loads[6].wait()
    loads[7].wait()
    loads[8].wait()

    step = 16

    def rows_of(h, i):
        return pl.ds(pl.multiple_of(h * part_points + i * step, step), step)

    def spread(k, rows):
        return jnp.concatenate([live[k, rows, :]] * (features // LANES), axis=1)

    def forward(h):
        span = pl.ds(h * part_points, part_points)
        for m in range(0, part_points, 128):
            rows = pl.ds(h * part_points + m, 128)
            for n in range(0, features, 256):
                lanes = pl.ds(n, 256)
                base = grid_proj[rows, lanes]
                v = dot(one_hot[0, rows, :], slot_proj[:, lanes]) + base
                pre[0, rows, lanes] = v
                total = silu(v)
                for k in range(1, per_point):
                    v = dot(one_hot[k, rows, :], slot_proj[:, lanes]) + base
                    pre[k, rows, lanes] = v
                    mask = jnp.concatenate([live[k, rows, :]] * 2, axis=1)
                    total += silu(v) * mask
                summed_act[rows, lanes] = total.astype(BF16)

        node_in = (
            dot(summed_act[span, :], w_msg[...]) + emb[span, :].astype(F32)
        ).astype(BF16)
        v = dot(node_in, w_node[...])
        node_pre[span, :] = v
        hidden = silu(v).astype(BF16)
        pred[h] = dot_t(hidden, w_out[...]).reshape(pred.shape[1:]).astype(BF16)

        pred_in[h, 0] = pred[h, ens]

        for to, q in ens_peers:
            remote(pred.at[h, to], pred_in.at[h, n_ens - q], 1 + h, {"ens": to}).start()

    def slopes(h):
        @pl.loop(0, part_points // step)
        def _(i):
            rows = rows_of(h, i)
            base = grid_proj[rows, :]
            for k in range(per_point):
                pre[k, rows, :] = slope(pre[k, rows, :])
            node_pre[rows, :] = slope(node_pre[rows, :])

    def scores(h):
        whole(pred_in.at[h, pl.ds(1, n_ens - 1)], 1 + h).wait_recv()
        pred_wide[...] = pred_in[h].astype(F32)
        share = part_points // n_ens

        @pl.loop(0, share // 8)
        def _(i):
            rows = pl.ds(pl.multiple_of(i * 8, 8), 8)
            goal = target[
                pl.ds(pl.multiple_of(h * part_points + ens * share + i * 8, 8), 8), :
            ]
            mine = [pred_wide[m, rows, :] for m in range(n_ens)]
            pairwise = [jnp.zeros_like(goal) for _ in range(n_ens)]
            for a in range(n_ens):
                for b in range(a + 1, n_ens):
                    t = mine[a] - mine[b]
                    g = t * lax.rsqrt(t * t + SOFT)
                    pairwise[a] += g
                    pairwise[b] -= g
            weight_row = var_wide[0:1, :]
            for m in range(n_ens):
                t = mine[m] - goal
                g = t * lax.rsqrt(t * t + SOFT)
                grad_wide[m, rows, :] = weight_row * (g - pairwise[m] * (1.0 / (n_ens - 1.0)))

        grad_out[h] = grad_wide[...].astype(BF16)
        grad_in[h, 0] = grad_out[h, 0]

        for to, q in ens_peers:
            remote(
                grad_out.at[h, q], grad_in.at[h, n_ens - q], 1 + PARTS + h, {"ens": to}
            ).start()

    def edge_backward(h):
        whole(grad_in.at[h, pl.ds(1, n_ens - 1)], 1 + PARTS + h).wait_recv()

        @pl.loop(0, n_ens)
        def _(q):
            pred_grad[h, lax.rem(ens + q, n_ens)] = grad_in[h, q]

        span = pl.ds(h * part_points, part_points)
        hidden_grad = (
            dot(pred_grad[h].reshape(part_points, LANES), w_out[...]) * node_pre[span, :]
        ).astype(BF16)
        edge_grad[h] = dot_t(hidden_grad, w_node[...]).astype(BF16)

    def weight_half(which, h):
        return dot(summed_act_t[which, :, h * part_points : (h + 1) * part_points], edge_grad[h])

    def slot_backward(h):
        @pl.loop(0, part_points // step)
        def _(i):
            rows = rows_of(h, i)
            b = back[pl.ds(pl.multiple_of(i * step, step), step), :]
            for k in range(per_point):
                pre_grad[
                    pl.ds(pl.multiple_of(k * part_points + i * step, step), step), :
                ] = (b * pre[k, rows, :]).astype(BF16)

    whole(in_rows.at[pl.ds(1, n_sp - 1)], 0).wait_recv()
    arrived = from_blocks(in_rows[...].astype(F32)).astype(BF16)
    slot_proj[...] = dot(arrived, w_send[...]).astype(BF16)
    for h in range(PARTS):
        forward(h)

    for h in range(PARTS):
        slopes(h)
    turned = jnp.transpose(summed_act[...].astype(F32)).reshape(n_sp, 2, features // n_sp // 2, points)
    for c in range(2):
        summed_act_t[c] = turned[:, c].reshape(half, points).astype(BF16)

    for h in range(PARTS):
        scores(h)

    theirs, ours = 1 - core, core
    for h in range(PARTS - 1):
        edge_backward(h)
        for i, which in enumerate((theirs, ours)):
            term = weight_half(which, h)
            halves[i] = term if h == 0 else halves[i] + term

    last = PARTS - 1
    edge_backward(last)
    pair_out[...] = (halves[0] + weight_half(theirs, last)).astype(BF16)
    pair = remote(pair_out, pair_in, 7, {"ens": ens + 1 - 2 * core})
    pair.start()
    own = halves[1] + weight_half(ours, last)
    halves[1] = own
    for h in range(PARTS):
        back[...] = dot_t(edge_grad[h], w_msg[...])
        slot_backward(h)
        if h < last:
            term = dot(one_hot_t[h], pre_grad[...])
            slot_grad[...] = term if h == 0 else slot_grad[...] + term
    pair.wait_recv()
    blocks = to_blocks(halves[1] + pair_in[...].astype(F32), n_sp).astype(BF16)
    sum_out[...] = blocks
    sum_in[0] = sum_out[sp]

    for to, _, back_place in space_peers:
        remote(sum_out.at[to], sum_in.at[back_place], 5, {"space": to}).start()

    blocks = to_blocks(
        slot_grad[...] + dot(one_hot_t[last], pre_grad[...]), n_sp
    ).astype(BF16)
    rows_out[...] = blocks
    rows_in[0] = blocks[0]
    space_exchange(rows_out, rows_in, 6)

    whole(sum_in.at[pl.ds(1, n_sp - 1)], 5).wait_recv()
    total_out[...] = jnp.sum(sum_in[...].astype(F32), axis=0).astype(BF16)
    total_in[0] = total_out[...]

    for to, q in ens_peers:
        remote(total_out, total_in.at[n_ens - q], 8, {"ens": to}).start()

    whole(rows_in.at[pl.ds(1, n_sp - 1)], 6).wait_recv()
    back_rows = from_blocks(rows_in[...].astype(F32)).astype(BF16)
    row_grads = dot(pick_t[...], back_rows)
    high = row_grads.astype(BF16)
    low = (row_grads - high.astype(F32)).astype(BF16)
    mesh_ref[...] = dot_t(high, w_send[...]) + dot_t(low, w_send[...])

    whole(total_in.at[pl.ds(1, n_ens - 1)], 8).wait_recv()
    same = total_in[0].astype(F32)
    other = total_in[1].astype(F32)
    for q in range(2, n_ens, 2):
        same += total_in[q].astype(F32)
        other += total_in[q + 1].astype(F32)
    first = jnp.where(core == 0, same, other)
    second = jnp.where(core == 0, other, same)
    weight_ref[...] = scale * jnp.concatenate(
        [from_blocks(first[None]), from_blocks(second[None])], axis=0
    )

    whole(out_rows.at[pl.ds(1, n_sp - 1)], 0).wait_send()
    for h in range(PARTS):
        whole(pred_in.at[h, pl.ds(1, n_ens - 1)], 1 + h).wait_send()
        whole(grad_out.at[h, pl.ds(1, n_ens - 1)], 1 + PARTS + h).wait_send()
    pair.wait_send()
    whole(sum_in.at[pl.ds(1, n_sp - 1)], 5).wait_send()
    whole(rows_out.at[pl.ds(1, n_sp - 1)], 6).wait_send()
    whole(total_in.at[pl.ds(1, n_ens - 1)], 8).wait_send()


def write_out(mesh_in, weight_in, mesh_ref, weight_ref, sem):
    copies = [
        pltpu.make_async_copy(mesh_in, mesh_ref, sem.at[0]),
        pltpu.make_async_copy(weight_in, weight_ref, sem.at[1]),
    ]
    for copy in copies:
        copy.start()
    for copy in copies:
        copy.wait()


def body(
    n_ens,
    n_sp,
    mesh_latent,
    grid_embed,
    w_send,
    w_recv,
    w_msg,
    w_node,
    w_out,
    target,
    var_weight,
    send_rows,
    edge_slot,
    edge_count,
):
    local_rows, features = mesh_latent.shape[1:]
    points, per_point = edge_slot.shape
    variables = target.shape[1]
    cap = send_rows.shape[2]
    slots = n_sp * cap
    part_points = points // PARTS
    share = part_points // n_ens
    half = features // 2
    out_block = features // n_sp
    total = n_ens * points * n_sp * per_point
    hbm = pl.BlockSpec(memory_space=pltpu.HBM)
    vmem = pl.BlockSpec(memory_space=pltpu.VMEM)
    square = (features, features)
    rows_blocks = (n_sp, 2 * cap, half)
    shares = (PARTS, n_ens, share, LANES)
    scratch = [
        pltpu.VMEM((local_rows, features), BF16),
        pltpu.VMEM((cap, n_sp), jnp.int32),
        pltpu.VMEM((points, features), BF16),
        pltpu.VMEM(square, BF16),
        pltpu.VMEM(square, BF16),
        pltpu.VMEM(square, BF16),
        pltpu.VMEM(square, BF16),
        pltpu.VMEM((variables, features), BF16),
        pltpu.VMEM((variables, points), F32),
        pltpu.VMEM((1, variables), F32),
        pltpu.VMEM((per_point, points), jnp.int32),
        pltpu.VMEM((1, points), jnp.int32),
        pltpu.VMEM((LANES, features), F32),
        pltpu.VMEM((LANES, features), BF16),
        pltpu.VMEM((LANES, points), F32),
        pltpu.VMEM((points, LANES), F32),
        pltpu.VMEM((8, LANES), F32),
        pltpu.VMEM((LANES, points), F32),
        pltpu.VMEM((points, LANES), F32),
        pltpu.VMEM((slots, local_rows), BF16),
        pltpu.VMEM((local_rows, slots), BF16),
        pltpu.VMEM(rows_blocks, BF16),
        pltpu.VMEM(rows_blocks, BF16),
        pltpu.VMEM((slots, features), BF16),
        pltpu.VMEM((points, features), F32),
        pltpu.VMEM((per_point, points, slots), BF16),
        pltpu.VMEM((PARTS, slots, per_point * part_points), BF16),
        pltpu.VMEM((per_point, points, features), F32),
        pltpu.VMEM((per_point, points, LANES), F32),
        pltpu.VMEM((points, features), BF16),
        pltpu.VMEM((2, half, points), BF16),
        pltpu.VMEM((points, features), F32),
        pltpu.VMEM(shares, BF16),
        pltpu.VMEM(shares, BF16),
        pltpu.VMEM(shares[1:], F32),
        pltpu.VMEM(shares[1:], F32),
        pltpu.VMEM(shares, BF16),
        pltpu.VMEM(shares, BF16),
        pltpu.VMEM(shares, BF16),
        pltpu.VMEM((PARTS, part_points, features), BF16),
        pltpu.VMEM((part_points, features), F32),
        pltpu.VMEM((per_point * part_points, features), BF16),
        pltpu.VMEM((slots, features), F32),
        pltpu.VMEM((2, half, features), F32),
        pltpu.VMEM((half, features), BF16),
        pltpu.VMEM((half, features), BF16),
        pltpu.VMEM((n_sp, out_block, half), BF16),
        pltpu.VMEM((n_sp, out_block, half), BF16),
        pltpu.VMEM((out_block, half), BF16),
        pltpu.VMEM((n_ens, out_block, half), BF16),
        pltpu.VMEM(rows_blocks, BF16),
        pltpu.VMEM(rows_blocks, BF16),
        pltpu.SemaphoreType.DMA((12,)),
        pltpu.SemaphoreType.DMA((9,)),
        pltpu.SemaphoreType.DMA((9,)),
    ]
    mesh_grad, weight_grad = pl.pallas_call(
        functools.partial(kernel, n_ens, n_sp, 1.0 / math.sqrt(total)),
        out_shape=(
            pltpu.VMEM((local_rows, features), F32),
            pltpu.VMEM((out_block, features), F32),
        ),
        in_specs=[hbm] * 12,
        out_specs=(vmem, vmem),
        scratch_shapes=scratch,
        compiler_params=pltpu.CompilerParams(
            collective_id=0, has_side_effects=True, vmem_limit_bytes=48 * 1024 * 1024
        ),
    )(
        *(
            pltpu.with_memory_space_constraint(array, pltpu.HBM)
            for array in (
                mesh_latent[0],
                grid_embed,
                w_send,
                w_recv,
                w_msg,
                w_node,
                w_out.T,
                target.T,
                var_weight.reshape(1, variables),
                jnp.swapaxes(send_rows[0], 0, 1),
                edge_slot.T,
                edge_count.reshape(1, points),
            )
        )
    )
    mesh_grad, weight_grad = pl.pallas_call(
        write_out,
        out_shape=(
            jax.ShapeDtypeStruct((local_rows, features), F32),
            jax.ShapeDtypeStruct((out_block, features), F32),
        ),
        in_specs=[vmem] * 2,
        out_specs=(hbm, hbm),
        scratch_shapes=[pltpu.SemaphoreType.DMA((2,))],
    )(
        pltpu.with_memory_space_constraint(mesh_grad, pltpu.VMEM),
        pltpu.with_memory_space_constraint(weight_grad, pltpu.VMEM),
    )
    return (mesh_grad[None], weight_grad)


def solution(mesh):
    in_specs = (
        P("ens", "space", None),
        P("space", None),
        P(),
        P(),
        P(),
        P(),
        P(),
        P("space", None),
        P(),
        P("space", None, None),
        P("space", None),
        P("space"),
    )
    out_specs = (P("ens", "space", None), P("space", None))
    return jax.shard_map(
        functools.partial(body, mesh.shape["ens"], mesh.shape["space"]),
        mesh=mesh,
        in_specs=in_specs,
        out_specs=out_specs,
        check_vma=False,
    )
```
